32 devices in a mesh: patch: 16 (over z, y, x), shard: 2 (over core).
Axes of the slice: x: 2, y: 2, z: 4, core: 2. Of those that a mesh axis runs over, the one named last changes fastest.
Arguments:
- node_latent: bfloat16 [4096, 512], P(('patch', 'shard')), may hold values from -6 to 6
- edge_latent: bfloat16 [32768, 512], P(('patch', 'shard')), may hold values from -6 to 6
- senders: int32 [32768], P(('patch', 'shard')), may hold values from 0 to 383
- receivers: int32 [32768], P(('patch', 'shard')), may hold values from 0 to 255
- halo_list: int32 [16, 128], P('patch'), may hold values from 0 to 255
- w_edge_first: bfloat16 [1536, 512], replicated, may hold values from -0.15625 to 0.15625
- w_edge_second: bfloat16 [512, 512], replicated, may hold values from -0.25 to 0.25
- w_node_first: bfloat16 [1024, 512], replicated, may hold values from -0.1875 to 0.1875
- w_node_second: bfloat16 [512, 512], replicated, may hold values from -0.25 to 0.25
- grad_node_new: bfloat16 [4096, 512], P(('patch', 'shard')), may hold values from -6 to 6
- grad_edge_new: bfloat16 [32768, 512], P(('patch', 'shard')), may hold values from -6 to 6
Outputs:
- grad_node_latent: bfloat16 [4096, 512], P(('patch', 'shard'))
- grad_edge_latent: bfloat16 [32768, 512], P(('patch', 'shard'))
- grad_edge_first: float32 [1536, 512], P(None, 'patch')
- grad_edge_second: float32 [512, 512], P(None, 'patch')
- grad_node_first: float32 [1024, 512], P(None, 'patch')
- grad_node_second: float32 [512, 512], P(None, 'patch')
The draws below stay inside these ranges and needn't reach their ends.
All inputs are finite; a program needn't handle non-finite values.
Results may differ from the reference program's by a relative error of at most 0.03.
Values may be sent and summed in bfloat16 or wider, within the bound.
A program may use at most 128 MiB of HBM per device.

```python
import jax
import jax.numpy as jnp
from jax import lax

D = 512
UNITS = 512
EDGE_DEV = 1024
NODE_DEV = 128
PATCH_NODES = 256
HALO = 64
NODES = 4096
EDGES = 32768
N_PATCH = 16
N_SHARD = 2


def plant(values, rng, smallest, top_value):
    longest = values.shape.index(max(values.shape))
    spots = []
    for shift in (0, 1):
        where = [jax.random.randint(jax.random.fold_in(rng, axis), (), 0, length) for axis, length in enumerate(values.shape)]
        where[longest] = (where[longest] + shift) % values.shape[longest]
        spots.append(tuple(where))
    return values.at[spots[0]].set(smallest).at[spots[1]].set(top_value)


def spiked(drawn, stream_key, source, target, shards_of, factor):
    owner, partner = [(jnp.arange(drawn.shape[axis_at]) // (drawn.shape[axis_at] // shards_of)).reshape([-1 if axis == axis_at else 1 for axis in range(drawn.ndim)]) for axis_at in (source, target)]
    chosen = jax.random.permutation(stream_key, shards_of)[partner]
    strong = (owner == chosen) | (owner == (partner + shards_of // 2) % shards_of)
    return jnp.where(strong, factor * drawn, drawn)


def shard_levels(key, extent, split, smallest, largest):
    level = 1.0
    for dim, blocks in split:
        draws = jax.random.uniform(jax.random.fold_in(jax.random.fold_in(key, 6), dim), (blocks,), jnp.float32, smallest / len(split), largest / len(split))
        level = level * jnp.repeat(jnp.exp(draws), extent[dim] // blocks).reshape((-1,) + (1,) * (len(extent) - 1 - dim))
    return level


def bell_draw(key, dims, spread, limit, pieces=(), dtype=jnp.bfloat16):
    gain = shard_levels(key, dims, pieces, -0.22, 0.18) if pieces else 1.0
    drawn = jax.random.normal(key, dims, jnp.float32) * spread * gain
    return jnp.minimum(jnp.maximum(drawn, -limit), limit).astype(dtype)


def heavy_noise(own_key, dims, spread, bound, pieces, heavy, dtype=jnp.bfloat16):
    entries = spread * jax.random.normal(own_key, dims, jnp.float32)
    if pieces:
        entries = entries * shard_levels(own_key, dims, pieces, -0.22, 0.18)
    return jnp.clip(spiked(entries, jax.random.fold_in(own_key, 3), *heavy), -bound, bound).astype(dtype)


def setup_inputs(seed: int = 0) -> dict:
    streams_of = jax.random.split(jax.random.key(seed), 12)
    node_latent = bell_draw(streams_of[0], (NODES, D), 1.0, 6.0, ((0, 32),))
    edge_latent = bell_draw(streams_of[1], (EDGES, D), 1.0, 6.0, ((0, 32),))
    senders = plant(jax.random.randint(streams_of[2], (EDGES,), 0, PATCH_NODES + 2 * HALO), jax.random.fold_in(streams_of[2], 1), 0, (PATCH_NODES + 2 * HALO) - 1).astype(jnp.int32)
    receivers = plant(jax.random.randint(streams_of[3], (EDGES,), 0, PATCH_NODES), jax.random.fold_in(streams_of[3], 1), 0, PATCH_NODES - 1).astype(jnp.int32)
    halo_list = plant(jax.random.randint(streams_of[4], (N_PATCH, 2 * HALO), 0, PATCH_NODES), jax.random.fold_in(streams_of[4], 1), 0, PATCH_NODES - 1).astype(jnp.int32)
    w_edge_first = bell_draw(streams_of[5], (3 * D, UNITS), (3 * D) ** -0.5, 0.15625)
    w_edge_second = bell_draw(streams_of[6], (UNITS, D), UNITS ** -0.5, 0.25)
    w_node_first = bell_draw(streams_of[7], (2 * D, UNITS), (2 * D) ** -0.5, 0.1875)
    w_node_second = bell_draw(streams_of[8], (UNITS, D), UNITS ** -0.5, 0.25)
    grad_node_new = heavy_noise(streams_of[9], (NODES, D), 1.0, 6.0, ((0, 32),), (0, 1, 32, 2.75))
    grad_edge_new = heavy_noise(streams_of[10], (EDGES, D), 1.0, 6.0, ((0, 32),), (0, 1, 32, 2.75))
    return dict(node_latent=node_latent, edge_latent=edge_latent, senders=senders, receivers=receivers, halo_list=halo_list, w_edge_first=w_edge_first, w_edge_second=w_edge_second, w_node_first=w_node_first, w_node_second=w_node_second, grad_node_new=grad_node_new, grad_edge_new=grad_edge_new)


epsilon = 1e-05

def swish_slope(values):
    sig = jax.nn.sigmoid(values)
    return sig * (1.0 + values * (1.0 - sig))

def contract_rows(left, right):
    return lax.dot_general(left, right, (((0,), (0,)), ((), ())), preferred_element_type=jnp.float32)

def times_transpose(left, right):
    return lax.dot_general(left, right, (((1,), (1,)), ((), ())), preferred_element_type=jnp.float32)

def mlp_forward(joined, w_first, w_second):
    pre_act = jnp.dot(joined, w_first, preferred_element_type=jnp.float32)
    activated = (pre_act * jax.nn.sigmoid(pre_act)).astype(jnp.bfloat16)
    output = jnp.dot(activated, w_second, preferred_element_type=jnp.float32)
    center = output - lax.optimization_barrier(jnp.mean(output, axis=-1, keepdims=True))
    inv_scale = lax.rsqrt(lax.optimization_barrier(jnp.mean(center * center, axis=-1, keepdims=True)) + epsilon)
    return (pre_act, activated, center * inv_scale, inv_scale)

def mlp_backward(joined, w_first, w_second, pre_act, activated, normed, inv_scale, cotangent):
    d_out = inv_scale * (cotangent - lax.optimization_barrier(jnp.mean(cotangent, axis=-1, keepdims=True)) - normed * lax.optimization_barrier(jnp.mean(cotangent * normed, axis=-1, keepdims=True)))
    d_out = d_out.astype(jnp.bfloat16)
    d_act = times_transpose(d_out, w_second)
    d_pre = (d_act * swish_slope(pre_act)).astype(jnp.bfloat16)
    grad_second = contract_rows(activated, d_out)
    grad_first = contract_rows(joined, d_pre)
    d_joined = times_transpose(d_pre, w_first)
    return (d_joined, grad_first, grad_second)

def reference(node_latent, edge_latent, senders, receivers, halo_list, w_edge_first, w_edge_second, w_node_first, w_node_second, grad_node_new, grad_edge_new):
    patch_rows = NODE_DEV * N_SHARD
    patch_edges = EDGE_DEV * N_SHARD
    nodes_all = node_latent.reshape(N_PATCH, patch_rows, D)
    outgoing = jax.vmap(lambda tab, idx: jnp.take(tab, idx, axis=0))(nodes_all, halo_list)
    from_prev = jnp.roll(outgoing[:, HALO:], 1, axis=0)
    from_next = jnp.roll(outgoing[:, :HALO], -1, axis=0)
    tables = jnp.concatenate([from_prev, nodes_all, from_next], axis=1)

    def one_patch(carry, items):
        table, own_nodes, edges, send_idx, recv_idx, node_cot, edge_cot = items
        joined = jnp.concatenate([edges, jnp.take(table, send_idx, axis=0), jnp.take(own_nodes, recv_idx, axis=0)], axis=1)
        pre_act, activated, normed, inv_scale = mlp_forward(joined, w_edge_first, w_edge_second)
        edge_new = (edges.astype(jnp.float32) + normed).astype(jnp.bfloat16)
        aggregate = jax.ops.segment_sum(edge_new.astype(jnp.float32), recv_idx, num_segments=patch_rows).astype(jnp.bfloat16)
        node_joined = jnp.concatenate([own_nodes, aggregate], axis=1)
        n_pre, n_act, n_normed, n_inv = mlp_forward(node_joined, w_node_first, w_node_second)
        node_grad = node_cot.astype(jnp.float32)
        d_node, g_node_first, g_node_second = mlp_backward(node_joined, w_node_first, w_node_second, n_pre, n_act, n_normed, n_inv, node_grad)
        d_aggregate = d_node[:, D:]
        edge_grad = edge_cot.astype(jnp.float32) + jnp.take(d_aggregate, recv_idx, axis=0)
        d_edge, g_edge_first, g_edge_second = mlp_backward(joined, w_edge_first, w_edge_second, pre_act, activated, normed, inv_scale, edge_grad)
        grad_edges = (edge_grad + d_edge[:, :D]).astype(jnp.bfloat16)
        sender_part = jax.ops.segment_sum(d_edge[:, D:2 * D], send_idx, num_segments=patch_rows + 2 * HALO)
        receiver_part = jax.ops.segment_sum(d_edge[:, 2 * D:], recv_idx, num_segments=patch_rows)
        own_part = sender_part[HALO:HALO + patch_rows] + receiver_part + node_grad + d_node[:, :D]
        back_part = jnp.concatenate([sender_part[:HALO], sender_part[HALO + patch_rows:]], axis=0)
        carry = (carry[0] + g_edge_first, carry[1] + g_edge_second, carry[2] + g_node_first, carry[3] + g_node_second)
        return (carry, (grad_edges, own_part, back_part))
    start = (jnp.zeros((3 * D, UNITS), jnp.float32), jnp.zeros((UNITS, D), jnp.float32), jnp.zeros((2 * D, UNITS), jnp.float32), jnp.zeros((UNITS, D), jnp.float32))
    items = (tables, nodes_all, edge_latent.reshape(N_PATCH, patch_edges, D), senders.reshape(N_PATCH, patch_edges), receivers.reshape(N_PATCH, patch_edges), grad_node_new.reshape(N_PATCH, patch_rows, D), grad_edge_new.reshape(N_PATCH, patch_edges, D))
    sums, (grad_edges, own_parts, back_parts) = lax.scan(one_patch, start, items)
    recv_prev = jnp.roll(back_parts[:, HALO:], 1, axis=0)
    recv_next = jnp.roll(back_parts[:, :HALO], -1, axis=0)

    def add_back(own_part, idx, got_prev, got_next):
        return own_part.at[idx[:HALO]].add(got_prev).at[idx[HALO:]].add(got_next)
    own_parts = jax.vmap(add_back)(own_parts, halo_list, recv_prev, recv_next)
    grad_node_latent = own_parts.reshape(N_PATCH * patch_rows, D).astype(jnp.bfloat16)
    grad_edge_latent = grad_edges.reshape(N_PATCH * patch_edges, D)
    return (grad_node_latent, grad_edge_latent, sums[0], sums[1], sums[2], sums[3])
```

```python
import functools

import jax
import jax.numpy as jnp
from jax import lax
from jax.experimental import pallas as pl
from jax.experimental.pallas import tpu as pltpu
from jax.sharding import PartitionSpec as P

epsilon = 1e-05
LANES = 128
bf16 = jnp.bfloat16
f32 = jnp.float32
MESH = pl.DeviceIdType.MESH


def padded(block, sides, width):
    for axis, dim in sides:
        count = lax.axis_size(axis)
        forward = [(i, i + 1) for i in range(count - 1)]
        forward.append((count - 1, 0))
        backward = [(target, source) for source, target in forward]
        low = lax.ppermute(
            lax.slice_in_dim(block, block.shape[dim] - width, None, axis=dim), axis, forward
        )
        high = lax.ppermute(lax.slice_in_dim(block, 0, width, axis=dim), axis, backward)
        block = jnp.concatenate([low, block, high], axis=dim)
    return block


def swish_slope(values):
    sig = jax.nn.sigmoid(values)
    return sig * (1.0 + values * (1.0 - sig))


def contract_rows(left, right):
    return lax.dot_general(
        left, right, (((0,), (0,)), ((), ())), preferred_element_type=jnp.float32
    )


def times_transpose(left, right):
    return lax.dot_general(
        left, right, (((1,), (1,)), ((), ())), preferred_element_type=jnp.float32
    )


def times(left, right):
    return jnp.dot(left, right, preferred_element_type=jnp.float32)


def layer_norm(output):
    center = output - jnp.mean(output, axis=-1, keepdims=True)
    inv_scale = lax.rsqrt(jnp.mean(center * center, axis=-1, keepdims=True) + epsilon)
    return center * inv_scale, inv_scale


def norm_backward(cotangent, normed, inv_scale):
    return (
        inv_scale
        * (
            cotangent
            - jnp.mean(cotangent, axis=-1, keepdims=True)
            - normed * jnp.mean(cotangent * normed, axis=-1, keepdims=True)
        )
    ).astype(bf16)


def mlp_forward(joined, w_first, w_second):
    pre_act = times(joined, w_first)
    activated = (pre_act * jax.nn.sigmoid(pre_act)).astype(jnp.bfloat16)
    normed, inv_scale = layer_norm(times(activated, w_second))
    return (pre_act, activated, normed, inv_scale)


def mlp_backward(joined, w_first, w_second, pre_act, activated, normed, inv_scale, cotangent):
    d_out = norm_backward(cotangent, normed, inv_scale)
    d_act = times_transpose(d_out, w_second)
    d_pre = (d_act * swish_slope(pre_act)).astype(jnp.bfloat16)
    grad_second = contract_rows(activated, d_out)
    grad_first = contract_rows(joined, d_pre)
    d_joined = times_transpose(d_pre, w_first)
    return (d_joined, grad_first, grad_second)


def general_body(
    node_latent,
    edge_latent,
    senders,
    receivers,
    halo_list,
    w_edge_first,
    w_edge_second,
    w_node_first,
    w_node_second,
    grad_node_new,
    grad_edge_new,
):
    shards = lax.axis_size("shard")
    node_rows = node_latent.shape[0]
    width = node_latent.shape[1]
    patch_rows = node_rows * shards
    send_lists = halo_list[0]
    halo_width = send_lists.shape[0] // 2
    gathered = lax.all_gather(node_latent, "shard", axis=0, tiled=True)
    outgoing = jnp.take(gathered, send_lists, axis=0)
    widened = padded(outgoing, (("patch", 0),), halo_width)
    from_prev = widened[:halo_width]
    from_next = widened[halo_width * 3 :]
    extended = jnp.concatenate([from_prev, gathered, from_next], axis=0)
    joined = jnp.concatenate(
        [edge_latent, jnp.take(extended, senders, axis=0), jnp.take(gathered, receivers, axis=0)],
        axis=1,
    )
    pre_act, activated, normed, inv_scale = mlp_forward(joined, w_edge_first, w_edge_second)
    edge_new = (edge_latent.astype(jnp.float32) + normed).astype(jnp.bfloat16)
    partial_value = jax.ops.segment_sum(
        edge_new.astype(jnp.float32), receivers, num_segments=patch_rows
    )
    aggregate = lax.psum_scatter(
        partial_value.astype(jnp.bfloat16), "shard", scatter_dimension=0, tiled=True
    )
    node_joined = jnp.concatenate([node_latent, aggregate], axis=1)
    n_pre, n_act, n_normed, n_inv = mlp_forward(node_joined, w_node_first, w_node_second)
    node_grad = grad_node_new.astype(jnp.float32)
    d_node, g_node_first, g_node_second = mlp_backward(
        node_joined, w_node_first, w_node_second, n_pre, n_act, n_normed, n_inv, node_grad
    )
    d_aggregate = d_node[:, width:]
    spread = lax.all_gather(d_aggregate.astype(jnp.bfloat16), "shard", axis=0, tiled=True).astype(
        d_aggregate.dtype
    )
    edge_grad = grad_edge_new.astype(jnp.float32) + jnp.take(spread, receivers, axis=0)
    d_edge, g_edge_first, g_edge_second = mlp_backward(
        joined, w_edge_first, w_edge_second, pre_act, activated, normed, inv_scale, edge_grad
    )
    grad_edge_latent = (edge_grad + d_edge[:, :width]).astype(jnp.bfloat16)
    sender_part = jax.ops.segment_sum(
        d_edge[:, width : 2 * width], senders, num_segments=patch_rows + 2 * halo_width
    )
    receiver_part = jax.ops.segment_sum(d_edge[:, 2 * width :], receivers, num_segments=patch_rows)
    back_part = jnp.concatenate(
        [sender_part[:halo_width], sender_part[halo_width + patch_rows :]], axis=0
    )
    returned = padded(back_part.astype(jnp.bfloat16), (("patch", 0),), halo_width).astype(
        back_part.dtype
    )
    own_rows = sender_part[halo_width : halo_width + patch_rows] + receiver_part
    own_rows = own_rows.at[send_lists[:halo_width]].add(returned[:halo_width])
    own_rows = own_rows.at[send_lists[halo_width:]].add(returned[halo_width * 3 :])
    node_total = lax.psum_scatter(
        own_rows.astype(jnp.bfloat16), "shard", scatter_dimension=0, tiled=True
    ).astype(jnp.float32)
    grad_node_latent = (node_total + node_grad + d_node[:, :width]).astype(jnp.bfloat16)
    summed = lax.psum(
        (g_edge_first, g_edge_second, g_node_first, g_node_second), ("patch", "shard")
    )
    patches = lax.axis_size("patch")
    patch_index = lax.axis_index("patch")
    sliced = tuple(
        (
            lax.dynamic_slice_in_dim(
                matrix, patch_index * (matrix.shape[1] // patches), matrix.shape[1] // patches, 1
            )
            for matrix in summed
        )
    )
    return (grad_node_latent, grad_edge_latent, sliced[0], sliced[1], sliced[2], sliced[3])


def rows_hot(index_row, count):
    k = index_row.shape[1]
    return (lax.broadcasted_iota(jnp.int32, (count, k), 0) == index_row).astype(f32).astype(bf16)


def lanes_hot(index_row, count):
    k = index_row.shape[1]
    column = jnp.broadcast_to(index_row, (LANES, k)).T
    lane = lax.broadcasted_iota(jnp.int32, (k, LANES), 1)
    parts = [(column == lane + base).astype(f32).astype(bf16) for base in range(0, count, LANES)]
    return jnp.concatenate(parts, axis=1)


def make_plan(patches, width, units, tables):
    bits = patches.bit_length() - 1
    first = list(range(bits))
    second = [1, 0] + first[2:]
    third = first[2:] + [0, 1]
    edge_cols = (tables["edge_first"] + tables["edge_second"]) // 2
    node_cols = (tables["node_first"] + tables["node_second"]) // 2
    def cut(total, share):
        return total * share // 8 // LANES * LANES
    a = cut(edge_cols, 3)
    jobs = [
        dict(group="edge", lo=0, hi=a, order=first),
        dict(group="edge", lo=a, hi=2 * a, order=second),
        dict(group="edge", lo=2 * a, hi=edge_cols, order=third),
    ]
    b = cut(node_cols, 4)
    jobs += [
        dict(group="node", lo=0, hi=b, order=first),
        dict(group="node", lo=b, hi=node_cols, order=second),
    ]
    offset = 0
    for job in jobs:
        job["cols"] = job["hi"] - job["lo"]
        job["out"] = offset
        offset += job["cols"]
    place = {
        "edge_first": ("edge", 0),
        "edge_second": ("edge", tables["edge_first"] // 2),
        "node_first": ("node", 0),
        "node_second": ("node", tables["node_first"] // 2),
    }
    return jobs, place, offset


def fused_kernel(cfg, *refs):
    patches, rows_out, chunk, steps = cfg["patches"], cfg["rows_out"], cfg["chunk"], cfg["steps"]
    jobs, place, tables = cfg["jobs"], cfg["place"], cfg["tables"]
    (node_ref, edge_ref, snd_ref, rcv_ref, halo_ref, a_ref, b_ref, na_ref, nb_ref, gn_ref, ge_ref) = refs[:11]
    gnode_out, gedge_out, wsum_out = refs[11:14]
    (ext, pre, act, normed, inv, dout, dpre, agg_acc, s_acc, r_acc,
     halo_send, agg_send, agg_recv, spread, back_send, back_recv, own_acc, own_send, own_recv,
     dnode, fin, send_sem, recv_sem) = refs[14:37]
    buffers = refs[37:]

    patch = lax.axis_index("patch")
    core = lax.axis_index("shard")
    other = 1 - core
    nxt = lax.rem(patch + 1, patches)
    prv = lax.rem(patch + patches - 1, patches)
    node_rows, width = node_ref.shape
    own = 2 * node_rows
    halo = halo_send.shape[0] // 2
    total = own + 2 * halo
    bits = patches.bit_length() - 1

    def bit_of(k):
        return lax.rem(lax.div(patch, jnp.int32(1 << k)), jnp.int32(2))

    def across(k):
        return patch + (1 - 2 * bit_of(k)) * (1 << k)

    greet = [(patch, other), (nxt, core), (prv, core)] + [(across(k), core) for k in range(bits)]
    barrier = pltpu.get_barrier_semaphore()
    for target in greet:
        pl.semaphore_signal(barrier, inc=1, device_id=target, device_id_type=MESH)
    pl.semaphore_wait(barrier, len(greet))

    started = []

    def send(src, dst, target):
        k = len(started)
        copy = pltpu.make_async_remote_copy(
            src_ref=src, dst_ref=dst, send_sem=send_sem.at[k], recv_sem=recv_sem.at[k],
            device_id=target, device_id_type=MESH,
        )
        copy.start()
        started.append(copy)
        return copy

    state = []
    at = 0
    for job in jobs:
        state.append(dict(job, bufs=buffers[at : at + 2 + bits], copy=None, step=0, base=None))
        at += 2 + bits

    def position(job, p):
        return sum(((p >> b) & 1) << (bits - 1 - i) for i, b in enumerate(job["order"]))

    def keep(name, first_col, value):
        half = tables[name] // 2
        group, offset = place[name]
        value = value.astype(bf16)
        for unit in range(0, value.shape[1], LANES):
            column = first_col + unit
            side, local = column // half, offset + column % half
            for job in state:
                if job["group"] == group and job["lo"] <= local < job["hi"]:
                    lane = local - job["lo"]
                    for p in range(patches):
                        job["bufs"][0][side, position(job, p), :, lane : lane + LANES] = value[
                            p * rows_out : (p + 1) * rows_out, unit : unit + LANES
                        ]

    def begin(group):
        for job in state:
            if job["group"] == group:
                job["copy"] = send(job["bufs"][0].at[other], job["bufs"][1], (patch, other))
                job["step"], job["base"] = 0, 0

    def advance(group):
        for job in state:
            if job["group"] != group or job["step"] > bits:
                continue
            step, base, block = job["step"], job["base"], job["bufs"][0]
            got = job["bufs"][1 + step]
            job["copy"].wait_recv()
            length = patches >> step
            if step == bits:
                value = block[core, base].astype(f32) + got[0].astype(f32)
                fin[core, :, job["out"] : job["out"] + job["cols"]] = value
            else:
                half = length // 2
                bit = bit_of(job["order"][step])
                away, stay = (1 - bit) * half, bit * half

                def add(start):
                    where = pl.ds(base + start, half)
                    block[core, where] = (
                        block[core, where].astype(f32) + got[pl.ds(start, half)].astype(f32)
                    ).astype(bf16)

                add(away)
                job["copy"] = send(
                    block.at[core, pl.ds(base + away, half)],
                    job["bufs"][2 + step],
                    (across(job["order"][step]), core),
                )
                add(stay)
                job["base"] = base + stay
            job["step"] = step + 1

    mine = pl.ds(pl.multiple_of(halo + core * node_rows, 16), node_rows)
    ext[mine, :] = node_ref[...]
    to_core = send(node_ref, ext.at[mine], (patch, other))
    zero = jnp.zeros((own, width), f32)
    agg_acc[...] = zero
    r_acc[...] = zero
    s_acc[...] = jnp.zeros((total, width), f32)
    to_core.wait_recv()
    inner = slice(halo, halo + own)
    halo_send[...] = times(lanes_hot(halo_ref[...], own), ext[inner, :]).astype(bf16)
    to_prev = send(halo_send.at[pl.ds(0, halo)], ext.at[pl.ds(halo + own, halo)], (prv, core))
    to_next = send(halo_send.at[pl.ds(halo, halo)], ext.at[pl.ds(0, halo)], (nxt, core))

    def rows_of(i):
        return pl.ds(pl.multiple_of(i * chunk, chunk), chunk)

    @pl.loop(0, steps)
    def _(i):
        rows = rows_of(i)
        taken = times(lanes_hot(rcv_ref[i], own), ext[inner, :]).astype(bf16)
        pre[rows, :] = times(edge_ref[rows, :], a_ref[:width, :]) + times(taken, a_ref[2 * width :, :])

    to_prev.wait_recv()
    to_next.wait_recv()

    @pl.loop(0, steps)
    def _(i):
        rows = rows_of(i)
        taken = times(lanes_hot(snd_ref[i], total), ext[...]).astype(bf16)
        value = pre[rows, :] + times(taken, a_ref[width : 2 * width, :])
        pre[rows, :] = value
        hidden = (value * jax.nn.sigmoid(value)).astype(bf16)
        act[rows, :] = hidden
        scaled, scale = layer_norm(times(hidden, b_ref[...]))
        normed[rows, :] = scaled
        inv[rows, :] = scale
        updated = (edge_ref[rows, :].astype(f32) + scaled).astype(bf16)
        agg_acc[...] += times(rows_hot(rcv_ref[i], own), updated)

    away_nodes = pl.ds(pl.multiple_of(other * node_rows, 16), node_rows)
    own_nodes = pl.ds(pl.multiple_of(core * node_rows, 16), node_rows)
    agg_send[...] = agg_acc[away_nodes, :].astype(bf16)
    send(agg_send, agg_recv, (patch, other)).wait_recv()

    node = node_ref[...]
    aggregate = (agg_acc[own_nodes, :] + agg_recv[...].astype(f32)).astype(bf16)
    n_pre = times(node, na_ref[:width, :]) + times(aggregate, na_ref[width:, :])
    n_act = (n_pre * jax.nn.sigmoid(n_pre)).astype(bf16)
    n_normed, n_inv = layer_norm(times(n_act, nb_ref[...]))
    node_grad = gn_ref[...].astype(f32)
    n_dout = norm_backward(node_grad, n_normed, n_inv)
    n_dpre = (times_transpose(n_dout, nb_ref[...]) * swish_slope(n_pre)).astype(bf16)
    spread[own_nodes, :] = times_transpose(n_dpre, na_ref[width:, :]).astype(bf16)
    to_spread = send(spread.at[own_nodes], spread.at[own_nodes], (patch, other))
    keep("node_first", 0, contract_rows(n_dpre, node))
    keep("node_first", width, contract_rows(n_dpre, aggregate))
    keep("node_second", 0, contract_rows(n_dout, n_act))
    begin("node")
    dnode[...] = node_grad + times_transpose(n_dpre, na_ref[:width, :])
    to_spread.wait_recv()

    def backward(i):
        rows = rows_of(i)
        cotangent = ge_ref[rows, :].astype(f32) + times(lanes_hot(rcv_ref[i], own), spread[...])
        d_out = norm_backward(cotangent, normed[rows, :], inv[rows, :])
        dout[rows, :] = d_out
        d_pre = (times_transpose(d_out, b_ref[...]) * swish_slope(pre[rows, :])).astype(bf16)
        dpre[rows, :] = d_pre
        gedge_out[rows, :] = (cotangent + times_transpose(d_pre, a_ref[:width, :])).astype(bf16)
        s_acc[...] += times(rows_hot(snd_ref[i], total), d_pre)
        r_acc[...] += times(rows_hot(rcv_ref[i], own), d_pre)

    pl.loop(0, steps // 2)(backward)
    advance("node")
    pl.loop(steps // 2, steps)(backward)
    advance("node")

    from_s = s_acc[...].astype(bf16)
    from_r = r_acc[...].astype(bf16)
    keep("edge_first", 0, contract_rows(dpre[...], edge_ref[...]))
    keep("edge_first", width, contract_rows(from_s, ext[...]))
    keep("edge_first", 2 * width, contract_rows(from_r, ext[inner, :]))
    keep("edge_second", 0, contract_rows(dout[...], act[...]))
    begin("edge")
    advance("node")

    back_send[:halo, :] = times_transpose(from_s[:halo, :], a_ref[width : 2 * width, :]).astype(bf16)
    back_send[halo:, :] = times_transpose(from_s[halo + own :, :], a_ref[width : 2 * width, :]).astype(bf16)
    back_prev = send(back_send.at[pl.ds(0, halo)], back_recv.at[pl.ds(halo, halo)], (prv, core))
    back_next = send(back_send.at[pl.ds(halo, halo)], back_recv.at[pl.ds(0, halo)], (nxt, core))
    advance("edge")
    own_acc[...] = times_transpose(from_s[inner, :], a_ref[width : 2 * width, :]) + times_transpose(
        from_r, a_ref[2 * width :, :]
    )
    back_prev.wait_recv()
    back_next.wait_recv()
    own_acc[...] += times(rows_hot(halo_ref[...], own), back_recv[...])
    own_send[...] = own_acc[away_nodes, :].astype(bf16)
    to_own = send(own_send, own_recv, (patch, other))
    advance("node")
    advance("edge")
    to_own.wait_recv()
    gnode_out[...] = (own_acc[own_nodes, :] + own_recv[...].astype(f32) + dnode[...]).astype(bf16)
    for _ in range(bits + 1):
        advance("node")
        advance("edge")

    send(fin.at[core], fin.at[core], (patch, other)).wait_recv()
    wsum_out[...] = fin[...]
    for copy in started:
        copy.wait_send()


def fused_body(
    node_latent,
    edge_latent,
    senders,
    receivers,
    halo_list,
    w_edge_first,
    w_edge_second,
    w_node_first,
    w_node_second,
    grad_node_new,
    grad_edge_new,
):
    patches = lax.axis_size("patch")
    edges, width = edge_latent.shape
    node_rows = node_latent.shape[0]
    units = w_edge_first.shape[1]
    chunk = 256
    steps = edges // chunk
    halo2 = halo_list.shape[1]
    own = 2 * node_rows
    total = own + halo2
    rows_out = units // patches
    bits = patches.bit_length() - 1
    tables = {
        "edge_first": w_edge_first.shape[0],
        "edge_second": w_edge_second.shape[0],
        "node_first": w_node_first.shape[0],
        "node_second": w_node_second.shape[0],
    }
    jobs, place, columns = make_plan(patches, width, units, tables)
    cfg = dict(patches=patches, rows_out=rows_out, chunk=chunk, steps=steps, jobs=jobs, place=place, tables=tables)
    job_bufs = []
    for job in jobs:
        shape = (rows_out, job["cols"])
        job_bufs.append(pltpu.VMEM((2, patches) + shape, bf16))
        job_bufs.append(pltpu.VMEM((patches,) + shape, bf16))
        job_bufs += [pltpu.VMEM((patches >> (k + 1),) + shape, bf16) for k in range(bits)]
    copies = 9 + len(jobs) * (bits + 1)
    scratch = [
        pltpu.VMEM((total, width), bf16),
        pltpu.VMEM((edges, units), f32),
        pltpu.VMEM((edges, units), bf16),
        pltpu.VMEM((edges, width), f32),
        pltpu.VMEM((edges, 1), f32),
        pltpu.VMEM((edges, width), bf16),
        pltpu.VMEM((edges, units), bf16),
        pltpu.VMEM((own, width), f32),
        pltpu.VMEM((total, units), f32),
        pltpu.VMEM((own, units), f32),
        pltpu.VMEM((halo2, width), bf16),
        pltpu.VMEM((node_rows, width), bf16),
        pltpu.VMEM((node_rows, width), bf16),
        pltpu.VMEM((own, width), bf16),
        pltpu.VMEM((halo2, width), bf16),
        pltpu.VMEM((halo2, width), bf16),
        pltpu.VMEM((own, width), f32),
        pltpu.VMEM((node_rows, width), bf16),
        pltpu.VMEM((node_rows, width), bf16),
        pltpu.VMEM((node_rows, width), f32),
        pltpu.VMEM((2, rows_out, columns), f32),
        pltpu.SemaphoreType.DMA((copies,)),
        pltpu.SemaphoreType.DMA((copies,)),
    ] + job_bufs
    vmem = pl.BlockSpec(memory_space=pltpu.VMEM)
    gnode, gedge, wsum = pl.pallas_call(
        functools.partial(fused_kernel, cfg),
        out_shape=[
            jax.ShapeDtypeStruct((node_rows, width), bf16),
            jax.ShapeDtypeStruct((edges, width), bf16),
            jax.ShapeDtypeStruct((2, rows_out, columns), f32),
        ],
        in_specs=[vmem] * 11,
        out_specs=[vmem] * 3,
        scratch_shapes=scratch,
        compiler_params=pltpu.CompilerParams(
            collective_id=0, has_side_effects=True, vmem_limit_bytes=52 * 1024 * 1024
        ),
        name="layer_backward",
    )(
        node_latent,
        edge_latent,
        senders.reshape(steps, 1, chunk),
        receivers.reshape(steps, 1, chunk),
        halo_list,
        w_edge_first,
        w_edge_second,
        w_node_first,
        w_node_second,
        grad_node_new,
        grad_edge_new,
    )
    base = {group: min(j["out"] for j in jobs if j["group"] == group) for group in ("edge", "node")}

    def matrix(name):
        group, offset = place[name]
        low = base[group] + offset
        part = wsum[:, :, low : low + tables[name] // 2]
        return jnp.transpose(part, (0, 2, 1)).reshape(tables[name], rows_out)

    return (gnode, gedge) + tuple(matrix(name) for name in ("edge_first", "edge_second", "node_first", "node_second"))


def solution(mesh):
    in_specs = (
        P(("patch", "shard"), None),
        P(("patch", "shard"), None),
        P(("patch", "shard")),
        P(("patch", "shard")),
        P("patch", None),
        P(),
        P(),
        P(),
        P(),
        P(("patch", "shard"), None),
        P(("patch", "shard"), None),
    )
    out_specs = (
        P(("patch", "shard"), None),
        P(("patch", "shard"), None),
        P(None, "patch"),
        P(None, "patch"),
        P(None, "patch"),
        P(None, "patch"),
    )
    patches, shards = mesh.shape["patch"], mesh.shape["shard"]
    covered = shards == 2 and patches >= 4 and patches & (patches - 1) == 0
    body = fused_body if covered else general_body
    return jax.shard_map(body, mesh=mesh, in_specs=in_specs, out_specs=out_specs, check_vma=False)
```

```python
import functools

import jax
import jax.numpy as jnp
from jax import lax
from jax.experimental import pallas as pl
from jax.experimental.pallas import tpu as pltpu
from jax.sharding import PartitionSpec as P

epsilon = 1e-05
LANES = 128
bf16 = jnp.bfloat16
f32 = jnp.float32
MESH = pl.DeviceIdType.MESH


def padded(block, sides, width):
    for axis, dim in sides:
        count = lax.axis_size(axis)
        forward = [(i, i + 1) for i in range(count - 1)]
        forward.append((count - 1, 0))
        backward = [(target, source) for source, target in forward]
        low = lax.ppermute(
            lax.slice_in_dim(block, block.shape[dim] - width, None, axis=dim), axis, forward
        )
        high = lax.ppermute(lax.slice_in_dim(block, 0, width, axis=dim), axis, backward)
        block = jnp.concatenate([low, block, high], axis=dim)
    return block


def swish_slope(values):
    sig = jax.nn.sigmoid(values)
    return sig * (1.0 + values * (1.0 - sig))


def contract_rows(left, right):
    return lax.dot_general(
        left, right, (((0,), (0,)), ((), ())), preferred_element_type=jnp.float32
    )


def times_transpose(left, right):
    return lax.dot_general(
        left, right, (((1,), (1,)), ((), ())), preferred_element_type=jnp.float32
    )


def times(left, right):
    return jnp.dot(left, right, preferred_element_type=jnp.float32)


def layer_norm(output):
    center = output - jnp.mean(output, axis=-1, keepdims=True)
    inv_scale = lax.rsqrt(jnp.mean(center * center, axis=-1, keepdims=True) + epsilon)
    return center * inv_scale, inv_scale


def norm_backward(cotangent, normed, inv_scale):
    return (
        inv_scale
        * (
            cotangent
            - jnp.mean(cotangent, axis=-1, keepdims=True)
            - normed * jnp.mean(cotangent * normed, axis=-1, keepdims=True)
        )
    ).astype(bf16)


def mlp_forward(joined, w_first, w_second):
    pre_act = times(joined, w_first)
    activated = (pre_act * jax.nn.sigmoid(pre_act)).astype(jnp.bfloat16)
    normed, inv_scale = layer_norm(times(activated, w_second))
    return (pre_act, activated, normed, inv_scale)


def mlp_backward(joined, w_first, w_second, pre_act, activated, normed, inv_scale, cotangent):
    d_out = norm_backward(cotangent, normed, inv_scale)
    d_act = times_transpose(d_out, w_second)
    d_pre = (d_act * swish_slope(pre_act)).astype(jnp.bfloat16)
    grad_second = contract_rows(activated, d_out)
    grad_first = contract_rows(joined, d_pre)
    d_joined = times_transpose(d_pre, w_first)
    return (d_joined, grad_first, grad_second)


def general_body(
    node_latent,
    edge_latent,
    senders,
    receivers,
    halo_list,
    w_edge_first,
    w_edge_second,
    w_node_first,
    w_node_second,
    grad_node_new,
    grad_edge_new,
):
    shards = lax.axis_size("shard")
    node_rows = node_latent.shape[0]
    width = node_latent.shape[1]
    patch_rows = node_rows * shards
    send_lists = halo_list[0]
    halo_width = send_lists.shape[0] // 2
    gathered = lax.all_gather(node_latent, "shard", axis=0, tiled=True)
    outgoing = jnp.take(gathered, send_lists, axis=0)
    widened = padded(outgoing, (("patch", 0),), halo_width)
    from_prev = widened[:halo_width]
    from_next = widened[halo_width * 3 :]
    extended = jnp.concatenate([from_prev, gathered, from_next], axis=0)
    joined = jnp.concatenate(
        [edge_latent, jnp.take(extended, senders, axis=0), jnp.take(gathered, receivers, axis=0)],
        axis=1,
    )
    pre_act, activated, normed, inv_scale = mlp_forward(joined, w_edge_first, w_edge_second)
    edge_new = (edge_latent.astype(jnp.float32) + normed).astype(jnp.bfloat16)
    partial_value = jax.ops.segment_sum(
        edge_new.astype(jnp.float32), receivers, num_segments=patch_rows
    )
    aggregate = lax.psum_scatter(
        partial_value.astype(jnp.bfloat16), "shard", scatter_dimension=0, tiled=True
    )
    node_joined = jnp.concatenate([node_latent, aggregate], axis=1)
    n_pre, n_act, n_normed, n_inv = mlp_forward(node_joined, w_node_first, w_node_second)
    node_grad = grad_node_new.astype(jnp.float32)
    d_node, g_node_first, g_node_second = mlp_backward(
        node_joined, w_node_first, w_node_second, n_pre, n_act, n_normed, n_inv, node_grad
    )
    d_aggregate = d_node[:, width:]
    spread = lax.all_gather(d_aggregate.astype(jnp.bfloat16), "shard", axis=0, tiled=True).astype(
        d_aggregate.dtype
    )
    edge_grad = grad_edge_new.astype(jnp.float32) + jnp.take(spread, receivers, axis=0)
    d_edge, g_edge_first, g_edge_second = mlp_backward(
        joined, w_edge_first, w_edge_second, pre_act, activated, normed, inv_scale, edge_grad
    )
    grad_edge_latent = (edge_grad + d_edge[:, :width]).astype(jnp.bfloat16)
    sender_part = jax.ops.segment_sum(
        d_edge[:, width : 2 * width], senders, num_segments=patch_rows + 2 * halo_width
    )
    receiver_part = jax.ops.segment_sum(d_edge[:, 2 * width :], receivers, num_segments=patch_rows)
    back_part = jnp.concatenate(
        [sender_part[:halo_width], sender_part[halo_width + patch_rows :]], axis=0
    )
    returned = padded(back_part.astype(jnp.bfloat16), (("patch", 0),), halo_width).astype(
        back_part.dtype
    )
    own_rows = sender_part[halo_width : halo_width + patch_rows] + receiver_part
    own_rows = own_rows.at[send_lists[:halo_width]].add(returned[:halo_width])
    own_rows = own_rows.at[send_lists[halo_width:]].add(returned[halo_width * 3 :])
    node_total = lax.psum_scatter(
        own_rows.astype(jnp.bfloat16), "shard", scatter_dimension=0, tiled=True
    ).astype(jnp.float32)
    grad_node_latent = (node_total + node_grad + d_node[:, :width]).astype(jnp.bfloat16)
    summed = lax.psum(
        (g_edge_first, g_edge_second, g_node_first, g_node_second), ("patch", "shard")
    )
    patches = lax.axis_size("patch")
    patch_index = lax.axis_index("patch")
    sliced = tuple(
        (
            lax.dynamic_slice_in_dim(
                matrix, patch_index * (matrix.shape[1] // patches), matrix.shape[1] // patches, 1
            )
            for matrix in summed
        )
    )
    return (grad_node_latent, grad_edge_latent, sliced[0], sliced[1], sliced[2], sliced[3])


def rows_hot(index_row, count):
    k = index_row.shape[1]
    return (lax.broadcasted_iota(jnp.int32, (count, k), 0) == index_row).astype(f32).astype(bf16)


def lanes_hot(index_row, count):
    k = index_row.shape[1]
    column = jnp.broadcast_to(index_row, (LANES, k)).T
    lane = lax.broadcasted_iota(jnp.int32, (k, LANES), 1)
    parts = [(column == lane + base).astype(f32).astype(bf16) for base in range(0, count, LANES)]
    return jnp.concatenate(parts, axis=1)


JOBS = ("node_first", "node_first", "node_second", "edge_second", "edge_first", "edge_first", "edge_first")


def make_orders(bits):
    upper = list(range(2, bits))
    first = [0, 1] + upper
    second = [1, 0] + upper
    third = upper + [0, 1]
    return (first, second, first, third, first, second, second)


def fused_kernel(cfg, *refs):
    patches, rows_out, half, chunk = cfg["patches"], cfg["rows_out"], cfg["half"], cfg["chunk"]
    (node_hbm, edge_hbm, snd_ref, rcv_ref, halo_ref, a_hbm, b_hbm, na_hbm, nb_hbm, gn_hbm, ge_hbm) = refs[:11]
    gnode_out, gedge_hbm, wsum_out = refs[11:14]
    (edge_ref, a_ref, b_ref, na_ref, nb_ref, gn_ref, ge_ref,
     ext, hot_s, hot_r, pre, act, normed, inv, cot, dout, dpre, dpre_t, updated, gedge,
     halo_send, agg_send, agg_recv, agg, n_dpre, n_dout, n_act, spread, dnode,
     back_send, back_recv, own_acc, own_send, own_recv, fin,
     in_sem, out_sem, send_sem, recv_sem) = refs[14:53]
    buffers = refs[53:]

    patch = lax.axis_index("patch")
    core = lax.axis_index("shard")
    other = 1 - core
    nxt = lax.rem(patch + 1, patches)
    prv = lax.rem(patch + patches - 1, patches)
    node_rows, width = node_hbm.shape
    edges = edge_hbm.shape[0]
    own = 2 * node_rows
    halo = halo_send.shape[0] // 2
    total = own + 2 * halo
    bits = patches.bit_length() - 1
    chunks = [slice(i, i + chunk) for i in range(0, edges, chunk)]

    def bit_of(k):
        return lax.rem(lax.div(patch, jnp.int32(1 << k)), jnp.int32(2))

    def across(k):
        return patch + (1 - 2 * bit_of(k)) * (1 << k)

    greet = [(patch, other), (nxt, core), (prv, core)] + [(across(k), core) for k in range(bits)]
    barrier = pltpu.get_barrier_semaphore()
    for target in greet:
        pl.semaphore_signal(barrier, inc=1, device_id=target, device_id_type=MESH)

    mine = pl.ds(pl.multiple_of(halo + core * node_rows, 16), node_rows)
    own_nodes = pl.ds(pl.multiple_of(core * node_rows, 16), node_rows)
    away_nodes = pl.ds(pl.multiple_of(other * node_rows, 16), node_rows)
    inner = slice(halo, halo + own)

    loads = {}
    for k, (name, src, dst) in enumerate(
        (
            ("node", node_hbm, ext.at[mine]),
            ("edge", edge_hbm, edge_ref),
            ("a", a_hbm, a_ref),
            ("b", b_hbm, b_ref),
            ("gn", gn_hbm, gn_ref.at[own_nodes]),
            ("na", na_hbm, na_ref),
            ("nb", nb_hbm, nb_ref),
            ("ge", ge_hbm, ge_ref),
        )
    ):
        loads[name] = pltpu.make_async_copy(src, dst, in_sem.at[k])
        loads[name].start()

    pl.semaphore_wait(barrier, len(greet))

    started = []

    def send(src, dst, target):
        k = len(started)
        copy = pltpu.make_async_remote_copy(
            src_ref=src, dst_ref=dst, send_sem=send_sem.at[k], recv_sem=recv_sem.at[k],
            device_id=target, device_id_type=MESH,
        )
        copy.start()
        started.append(copy)
        return copy

    to_core = send(node_hbm, ext.at[mine], (patch, other))
    to_core_grad = send(gn_hbm, gn_ref.at[own_nodes], (patch, other))

    state = []
    for k, order in enumerate(make_orders(bits)):
        bufs = buffers[k * (2 + bits) : (k + 1) * (2 + bits)]
        state.append(dict(order=order, bufs=bufs, copy=None, step=0, base=0, out=k * half))

    def gradient(k, left_t, right):
        job = state[k]
        block = job["bufs"][0]
        for side in (other, core):
            lanes = pl.ds(pl.multiple_of(side * half, LANES), half)
            value = times(left_t, right(lanes)).astype(bf16)
            for p in range(patches):
                where = sum(((p >> b) & 1) << (bits - 1 - i) for i, b in enumerate(job["order"]))
                block[side, where] = value[p * rows_out : (p + 1) * rows_out]
            if side is other:
                job["copy"] = send(block.at[other], job["bufs"][1], (patch, other))

    def advance(*ks):
        for k in ks:
            job = state[k]
            step, base, block = job["step"], job["base"], job["bufs"][0]
            if step > bits:
                continue
            got = job["bufs"][1 + step]
            job["copy"].wait_recv()
            if step == bits:
                value = block[core, base].astype(f32) + got[0].astype(f32)
                fin[core, :, job["out"] : job["out"] + half] = value
            else:
                count = (patches >> step) // 2
                bit = bit_of(job["order"][step])
                away, stay = (1 - bit) * count, bit * count

                def add(start):
                    where = pl.ds(base + start, count)
                    block[core, where] = (
                        block[core, where].astype(f32) + got[pl.ds(start, count)].astype(f32)
                    ).astype(bf16)

                add(away)
                job["copy"] = send(
                    block.at[core, pl.ds(base + away, count)],
                    job["bufs"][2 + step],
                    (across(job["order"][step]), core),
                )
                add(stay)
                job["base"] = base + stay
            job["step"] = step + 1

    hot_r[...] = lanes_hot(rcv_ref[...], own)
    loads["edge"].wait()
    loads["a"].wait()
    for rows in chunks:
        pre[rows, :] = times(edge_ref[rows, :], a_ref[:width, :])
    loads["node"].wait()
    to_core.wait_recv()
    halo_send[...] = times(lanes_hot(halo_ref[...], own), ext[inner, :]).astype(bf16)
    to_prev = send(halo_send.at[pl.ds(0, halo)], ext.at[pl.ds(halo + own, halo)], (prv, core))
    to_next = send(halo_send.at[pl.ds(halo, halo)], ext.at[pl.ds(0, halo)], (nxt, core))

    for rows in chunks:
        taken = times(hot_r[rows, :], ext[inner, :]).astype(bf16)
        pre[rows, :] += times(taken, a_ref[2 * width :, :])
    hot_s[...] = lanes_hot(snd_ref[...], total)
    loads["b"].wait()
    to_prev.wait_recv()
    to_next.wait_recv()
    for rows in chunks:
        taken = times(hot_s[rows, :], ext[...]).astype(bf16)
        value = pre[rows, :] + times(taken, a_ref[width : 2 * width, :])
        pre[rows, :] = value
        hidden = (value * jax.nn.sigmoid(value)).astype(bf16)
        act[rows, :] = hidden
        scaled, scale = layer_norm(times(hidden, b_ref[...]))
        normed[rows, :] = scaled
        inv[rows, :] = scale
        updated[rows, :] = (edge_ref[rows, :].astype(f32) + scaled).astype(bf16)
    agg_send[...] = times(rows_hot(rcv_ref[...], own), updated[...]).astype(bf16)
    to_agg = send(agg_send, agg_recv, (patch, other))

    @pl.loop(0, edges // LANES)
    def _(i):
        rows = pl.ds(pl.multiple_of(i * LANES, LANES), LANES)
        pre[rows, :] = swish_slope(pre[rows, :])

    for name in ("na", "nb", "gn", "ge"):
        loads[name].wait()
    to_core_grad.wait_recv()
    to_agg.wait_recv()

    node = ext[inner, :]
    aggregate = (agg_send[...].astype(f32) + agg_recv[...].astype(f32)).astype(bf16)
    agg[...] = aggregate
    n_pre = times(node, na_ref[:width, :]) + times(aggregate, na_ref[width:, :])
    hidden = (n_pre * jax.nn.sigmoid(n_pre)).astype(bf16)
    n_act[...] = hidden
    n_normed, n_inv = layer_norm(times(hidden, nb_ref[...]))
    d_out = norm_backward(gn_ref[...].astype(f32), n_normed, n_inv)
    n_dout[...] = d_out
    d_pre = (times_transpose(d_out, nb_ref[...]) * swish_slope(n_pre)).astype(bf16)
    n_dpre[...] = d_pre
    spread[...] = times_transpose(d_pre, na_ref[width:, :]).astype(bf16)

    n_dpre_own = n_dpre[own_nodes, :]
    n_dpre_t = n_dpre_own.T
    gradient(0, n_dpre_t, lambda lanes: ext[mine, lanes])
    gradient(1, n_dpre_t, lambda lanes: agg[own_nodes, lanes])
    gradient(2, n_dout[own_nodes, :].T, lambda lanes: n_act[own_nodes, lanes])

    for rows in chunks:
        cotangent = ge_ref[rows, :].astype(f32) + times(hot_r[rows, :], spread[...])
        cot[rows, :] = cotangent
        dout[rows, :] = norm_backward(cotangent, normed[rows, :], inv[rows, :])
    advance(0, 1, 2)
    gradient(3, dout[...].T, lambda lanes: act[:, lanes])
    for rows in chunks:
        dpre[rows, :] = (times_transpose(dout[rows, :], b_ref[...]) * pre[rows, :]).astype(bf16)
    dpre_t[...] = dpre[...].T
    advance(3)
    gradient(4, dpre_t[...], lambda lanes: edge_ref[:, lanes])
    from_s_t = times(dpre_t[...], hot_s[...]).astype(bf16)
    gradient(5, from_s_t, lambda lanes: ext[:, lanes])
    from_r_t = times(dpre_t[...], hot_r[...]).astype(bf16)
    gradient(6, from_r_t, lambda lanes: ext[inner, lanes])
    advance(4, 0, 1, 2)

    from_s = from_s_t.T
    from_r = from_r_t.T
    back_send[:halo, :] = times_transpose(from_s[:halo, :], a_ref[width : 2 * width, :]).astype(bf16)
    back_send[halo:, :] = times_transpose(from_s[halo + own :, :], a_ref[width : 2 * width, :]).astype(bf16)
    back_prev = send(back_send.at[pl.ds(0, halo)], back_recv.at[pl.ds(halo, halo)], (prv, core))
    back_next = send(back_send.at[pl.ds(halo, halo)], back_recv.at[pl.ds(0, halo)], (nxt, core))
    advance(5, 6)
    stores = []

    def edge_rows(k):
        rows = chunks[k]
        gedge[rows, :] = (cot[rows, :] + times_transpose(dpre[rows, :], a_ref[:width, :])).astype(bf16)
        stores.append(pltpu.make_async_copy(gedge.at[rows], gedge_hbm.at[rows], out_sem.at[k]))
        stores[-1].start()

    split = len(chunks) // 2
    for k in range(split):
        edge_rows(k)
    advance(3, 4, 0, 1, 2)
    for k in range(split, len(chunks)):
        edge_rows(k)
    own_acc[...] = times_transpose(from_s[inner, :], a_ref[width : 2 * width, :]) + times_transpose(
        from_r, a_ref[2 * width :, :]
    )
    dnode[...] = gn_ref[own_nodes, :].astype(f32) + times_transpose(n_dpre_own, na_ref[:width, :])
    advance(5, 6, 3, 4)
    back_prev.wait_recv()
    back_next.wait_recv()
    own_acc[...] += times(rows_hot(halo_ref[...], own), back_recv[...])
    own_send[...] = own_acc[away_nodes, :].astype(bf16)
    to_own = send(own_send, own_recv, (patch, other))
    advance(5, 6, 0, 1, 2, 3, 4)
    to_own.wait_recv()
    gnode_out[...] = (own_acc[own_nodes, :] + own_recv[...].astype(f32) + dnode[...]).astype(bf16)
    for _ in range(bits):
        advance(0, 1, 2, 3, 4, 5, 6)

    send(fin.at[core], fin.at[core], (patch, other)).wait_recv()
    wsum_out[...] = fin[...]
    for copy in stores:
        copy.wait()
    for copy in started:
        copy.wait_send()


def finish_kernel(half, gnode_ref, gedge_ref, wsum_ref, gnode_out, gedge_out, e1, e2, n1, n2, sem):
    copies = [(gedge_ref, gedge_out), (gnode_ref, gnode_out)]
    outs = {"edge_first": e1, "edge_second": e2, "node_first": n1, "node_second": n2}
    seen = {name: 0 for name in outs}
    for k, name in enumerate(JOBS):
        for side in range(2):
            low = seen[name] + side * half
            copies.append((wsum_ref.at[side, :, k * half : (k + 1) * half], outs[name].at[:, low : low + half]))
        seen[name] += 2 * half
    copies = [pltpu.make_async_copy(src, dst, sem.at[k]) for k, (src, dst) in enumerate(copies)]
    for copy in copies:
        copy.start()
    for copy in copies:
        copy.wait()


def fused_body(
    node_latent,
    edge_latent,
    senders,
    receivers,
    halo_list,
    w_edge_first,
    w_edge_second,
    w_node_first,
    w_node_second,
    grad_node_new,
    grad_edge_new,
):
    patches = lax.axis_size("patch")
    edges, width = edge_latent.shape
    node_rows = node_latent.shape[0]
    units = w_edge_first.shape[1]
    half = width // 2
    chunk = edges // 2
    halo2 = halo_list.shape[1]
    own = 2 * node_rows
    total = own + halo2
    rows_out = units // patches
    bits = patches.bit_length() - 1
    cfg = dict(patches=patches, rows_out=rows_out, half=half, chunk=chunk)
    job_bufs = []
    for _ in JOBS:
        shape = (rows_out, half)
        job_bufs.append(pltpu.VMEM((2, patches) + shape, bf16))
        job_bufs.append(pltpu.VMEM((patches,) + shape, bf16))
        job_bufs += [pltpu.VMEM((patches >> (k + 1),) + shape, bf16) for k in range(bits)]
    copies = 9 + len(JOBS) * (bits + 1)
    scratch = [
        pltpu.VMEM(edge_latent.shape, bf16),
        pltpu.VMEM(w_edge_first.shape, bf16),
        pltpu.VMEM(w_edge_second.shape, bf16),
        pltpu.VMEM(w_node_first.shape, bf16),
        pltpu.VMEM(w_node_second.shape, bf16),
        pltpu.VMEM((own, width), bf16),
        pltpu.VMEM((edges, width), bf16),
        pltpu.VMEM((total, width), bf16),
        pltpu.VMEM((edges, total), bf16),
        pltpu.VMEM((edges, own), bf16),
        pltpu.VMEM((edges, units), f32),
        pltpu.VMEM((edges, units), bf16),
        pltpu.VMEM((edges, width), f32),
        pltpu.VMEM((edges, 1), f32),
        pltpu.VMEM((edges, width), f32),
        pltpu.VMEM((edges, width), bf16),
        pltpu.VMEM((edges, units), bf16),
        pltpu.VMEM((units, edges), bf16),
        pltpu.VMEM((edges, width), bf16),
        pltpu.VMEM((edges, width), bf16),
        pltpu.VMEM((halo2, width), bf16),
        pltpu.VMEM((own, width), bf16),
        pltpu.VMEM((own, width), bf16),
        pltpu.VMEM((own, width), bf16),
        pltpu.VMEM((own, units), bf16),
        pltpu.VMEM((own, width), bf16),
        pltpu.VMEM((own, units), bf16),
        pltpu.VMEM((own, width), bf16),
        pltpu.VMEM((node_rows, width), f32),
        pltpu.VMEM((halo2, width), bf16),
        pltpu.VMEM((halo2, width), bf16),
        pltpu.VMEM((own, width), f32),
        pltpu.VMEM((node_rows, width), bf16),
        pltpu.VMEM((node_rows, width), bf16),
        pltpu.VMEM((2, rows_out, len(JOBS) * half), f32),
        pltpu.SemaphoreType.DMA((8,)),
        pltpu.SemaphoreType.DMA((edges // chunk,)),
        pltpu.SemaphoreType.DMA((copies,)),
        pltpu.SemaphoreType.DMA((copies,)),
    ] + job_bufs
    vmem = pl.BlockSpec(memory_space=pltpu.VMEM)
    hbm = pl.BlockSpec(memory_space=pltpu.HBM)
    anywhere = pl.BlockSpec(memory_space=pl.ANY)
    gnode, gedge, wsum = pl.pallas_call(
        functools.partial(fused_kernel, cfg),
        out_shape=[
            jax.ShapeDtypeStruct((node_rows, width), bf16),
            jax.ShapeDtypeStruct((edges, width), bf16),
            jax.ShapeDtypeStruct((2, rows_out, len(JOBS) * half), f32),
        ],
        in_specs=[hbm, hbm, vmem, vmem, vmem] + [hbm] * 6,
        out_specs=[vmem, anywhere, vmem],
        scratch_shapes=scratch,
        compiler_params=pltpu.CompilerParams(
            collective_id=0, has_side_effects=True, vmem_limit_bytes=56 * 1024 * 1024
        ),
        name="layer_backward",
    )(
        node_latent,
        edge_latent,
        senders.reshape(1, edges),
        receivers.reshape(1, edges),
        halo_list,
        w_edge_first,
        w_edge_second,
        w_node_first,
        w_node_second,
        grad_node_new,
        grad_edge_new,
    )
    matrices = (w_edge_first, w_edge_second, w_node_first, w_node_second)
    gnode, gedge, *parts = pl.pallas_call(
        functools.partial(finish_kernel, half),
        out_shape=[
            jax.ShapeDtypeStruct((node_rows, width), bf16),
            jax.ShapeDtypeStruct((edges, width), bf16),
        ]
        + [jax.ShapeDtypeStruct((rows_out, m.shape[0]), f32) for m in matrices],
        in_specs=[anywhere] * 3,
        out_specs=[hbm] * 6,
        scratch_shapes=[pltpu.SemaphoreType.DMA((2 + 2 * len(JOBS),))],
        name="results",
    )(gnode, gedge, wsum)
    return (gnode, gedge) + tuple(part.T for part in parts)


def solution(mesh):
    in_specs = (
        P(("patch", "shard"), None),
        P(("patch", "shard"), None),
        P(("patch", "shard")),
        P(("patch", "shard")),
        P("patch", None),
        P(),
        P(),
        P(),
        P(),
        P(("patch", "shard"), None),
        P(("patch", "shard"), None),
    )
    out_specs = (
        P(("patch", "shard"), None),
        P(("patch", "shard"), None),
        P(None, "patch"),
        P(None, "patch"),
        P(None, "patch"),
        P(None, "patch"),
    )
    patches, shards = mesh.shape["patch"], mesh.shape["shard"]
    covered = shards == 2 and patches >= 4 and patches & (patches - 1) == 0
    body = fused_body if covered else general_body
    return jax.shard_map(body, mesh=mesh, in_specs=in_specs, out_specs=out_specs, check_vma=False)
```

```python
import functools

import jax
import jax.numpy as jnp
from jax import lax
from jax.experimental import pallas as pl
from jax.experimental.pallas import tpu as pltpu
from jax.sharding import PartitionSpec as P

epsilon = 1e-05
LANES = 128
TILE = 32
bf16 = jnp.bfloat16
f32 = jnp.float32
MESH = pl.DeviceIdType.MESH


def padded(block, sides, width):
    for axis, dim in sides:
        count = lax.axis_size(axis)
        forward = [(i, i + 1) for i in range(count - 1)]
        forward.append((count - 1, 0))
        backward = [(target, source) for source, target in forward]
        low = lax.ppermute(
            lax.slice_in_dim(block, block.shape[dim] - width, None, axis=dim), axis, forward
        )
        high = lax.ppermute(lax.slice_in_dim(block, 0, width, axis=dim), axis, backward)
        block = jnp.concatenate([low, block, high], axis=dim)
    return block


def swish_slope(values):
    sig = jax.nn.sigmoid(values)
    return sig * (1.0 + values * (1.0 - sig))


def contract_rows(left, right):
    return lax.dot_general(
        left, right, (((0,), (0,)), ((), ())), preferred_element_type=jnp.float32
    )


def times_transpose(left, right):
    return lax.dot_general(
        left, right, (((1,), (1,)), ((), ())), preferred_element_type=jnp.float32
    )


def times(left, right):
    return jnp.dot(left, right, preferred_element_type=jnp.float32)


def layer_norm(output):
    center = output - jnp.mean(output, axis=-1, keepdims=True)
    inv_scale = lax.rsqrt(jnp.mean(center * center, axis=-1, keepdims=True) + epsilon)
    return center * inv_scale, inv_scale


def norm_backward(cotangent, normed, inv_scale):
    return (
        inv_scale
        * (
            cotangent
            - jnp.mean(cotangent, axis=-1, keepdims=True)
            - normed * jnp.mean(cotangent * normed, axis=-1, keepdims=True)
        )
    ).astype(bf16)


def mlp_forward(joined, w_first, w_second):
    pre_act = times(joined, w_first)
    activated = (pre_act * jax.nn.sigmoid(pre_act)).astype(jnp.bfloat16)
    normed, inv_scale = layer_norm(times(activated, w_second))
    return (pre_act, activated, normed, inv_scale)


def mlp_backward(joined, w_first, w_second, pre_act, activated, normed, inv_scale, cotangent):
    d_out = norm_backward(cotangent, normed, inv_scale)
    d_act = times_transpose(d_out, w_second)
    d_pre = (d_act * swish_slope(pre_act)).astype(jnp.bfloat16)
    grad_second = contract_rows(activated, d_out)
    grad_first = contract_rows(joined, d_pre)
    d_joined = times_transpose(d_pre, w_first)
    return (d_joined, grad_first, grad_second)


def general_body(
    node_latent,
    edge_latent,
    senders,
    receivers,
    halo_list,
    w_edge_first,
    w_edge_second,
    w_node_first,
    w_node_second,
    grad_node_new,
    grad_edge_new,
):
    shards = lax.axis_size("shard")
    node_rows = node_latent.shape[0]
    width = node_latent.shape[1]
    patch_rows = node_rows * shards
    send_lists = halo_list[0]
    halo_width = send_lists.shape[0] // 2
    gathered = lax.all_gather(node_latent, "shard", axis=0, tiled=True)
    outgoing = jnp.take(gathered, send_lists, axis=0)
    widened = padded(outgoing, (("patch", 0),), halo_width)
    from_prev = widened[:halo_width]
    from_next = widened[halo_width * 3 :]
    extended = jnp.concatenate([from_prev, gathered, from_next], axis=0)
    joined = jnp.concatenate(
        [edge_latent, jnp.take(extended, senders, axis=0), jnp.take(gathered, receivers, axis=0)],
        axis=1,
    )
    pre_act, activated, normed, inv_scale = mlp_forward(joined, w_edge_first, w_edge_second)
    edge_new = (edge_latent.astype(jnp.float32) + normed).astype(jnp.bfloat16)
    partial_value = jax.ops.segment_sum(
        edge_new.astype(jnp.float32), receivers, num_segments=patch_rows
    )
    aggregate = lax.psum_scatter(
        partial_value.astype(jnp.bfloat16), "shard", scatter_dimension=0, tiled=True
    )
    node_joined = jnp.concatenate([node_latent, aggregate], axis=1)
    n_pre, n_act, n_normed, n_inv = mlp_forward(node_joined, w_node_first, w_node_second)
    node_grad = grad_node_new.astype(jnp.float32)
    d_node, g_node_first, g_node_second = mlp_backward(
        node_joined, w_node_first, w_node_second, n_pre, n_act, n_normed, n_inv, node_grad
    )
    d_aggregate = d_node[:, width:]
    spread = lax.all_gather(d_aggregate.astype(jnp.bfloat16), "shard", axis=0, tiled=True).astype(
        d_aggregate.dtype
    )
    edge_grad = grad_edge_new.astype(jnp.float32) + jnp.take(spread, receivers, axis=0)
    d_edge, g_edge_first, g_edge_second = mlp_backward(
        joined, w_edge_first, w_edge_second, pre_act, activated, normed, inv_scale, edge_grad
    )
    grad_edge_latent = (edge_grad + d_edge[:, :width]).astype(jnp.bfloat16)
    sender_part = jax.ops.segment_sum(
        d_edge[:, width : 2 * width], senders, num_segments=patch_rows + 2 * halo_width
    )
    receiver_part = jax.ops.segment_sum(d_edge[:, 2 * width :], receivers, num_segments=patch_rows)
    back_part = jnp.concatenate(
        [sender_part[:halo_width], sender_part[halo_width + patch_rows :]], axis=0
    )
    returned = padded(back_part.astype(jnp.bfloat16), (("patch", 0),), halo_width).astype(
        back_part.dtype
    )
    own_rows = sender_part[halo_width : halo_width + patch_rows] + receiver_part
    own_rows = own_rows.at[send_lists[:halo_width]].add(returned[:halo_width])
    own_rows = own_rows.at[send_lists[halo_width:]].add(returned[halo_width * 3 :])
    node_total = lax.psum_scatter(
        own_rows.astype(jnp.bfloat16), "shard", scatter_dimension=0, tiled=True
    ).astype(jnp.float32)
    grad_node_latent = (node_total + node_grad + d_node[:, :width]).astype(jnp.bfloat16)
    summed = lax.psum(
        (g_edge_first, g_edge_second, g_node_first, g_node_second), ("patch", "shard")
    )
    patches = lax.axis_size("patch")
    patch_index = lax.axis_index("patch")
    sliced = tuple(
        (
            lax.dynamic_slice_in_dim(
                matrix, patch_index * (matrix.shape[1] // patches), matrix.shape[1] // patches, 1
            )
            for matrix in summed
        )
    )
    return (grad_node_latent, grad_edge_latent, sliced[0], sliced[1], sliced[2], sliced[3])


def rows_hot(index_row, count):
    k = index_row.shape[1]
    return (lax.broadcasted_iota(jnp.int32, (count, k), 0) == index_row).astype(f32).astype(bf16)


def lanes_hot(index_row, count):
    k = index_row.shape[1]
    column = jnp.broadcast_to(index_row, (LANES, k)).T
    lane = lax.broadcasted_iota(jnp.int32, (k, LANES), 1)
    parts = [(column == lane + base).astype(f32).astype(bf16) for base in range(0, count, LANES)]
    return jnp.concatenate(parts, axis=1)


JOBS = ("node_first", "node_first", "node_second", "edge_second", "edge_first", "edge_first", "edge_first")


def make_phases(bits):
    upper = list(range(2, bits))
    first = ([0], [1], upper)
    second = ([1], [0], upper)
    third = (upper, [0], [1])
    return (first, second, first, third, first, second, second)


def fused_kernel(cfg, *refs):
    patches, rows_out, half, chunk = cfg["patches"], cfg["rows_out"], cfg["half"], cfg["chunk"]
    (node_hbm, edge_hbm, snd_ref, rcv_ref, halo_ref, a_hbm, b_hbm, na_hbm, nb_hbm, gn_hbm, ge_hbm) = refs[:11]
    gnode_out, gedge_hbm, wsum_out = refs[11:14]
    (edge_ref, a_ref, b_ref, na_ref, nb_ref, gn_ref, ge_ref,
     ext, hot_s, hot_r, pre, act, normed, inv, cot, dout, dpre, dpre_t, updated, gedge,
     halo_send, agg_send, agg_recv, agg, n_dpre, n_dout, n_act, n_pre, n_out, spread, dnode,
     back_send, back_recv, own_acc, own_send, own_recv, fin,
     in_sem, out_sem, send_sem, recv_sem) = refs[14:55]
    buffers = refs[55:]

    patch = lax.axis_index("patch")
    core = lax.axis_index("shard")
    other = 1 - core
    nxt = lax.rem(patch + 1, patches)
    prv = lax.rem(patch + patches - 1, patches)
    node_rows, width = node_hbm.shape
    edges = edge_hbm.shape[0]
    own = 2 * node_rows
    halo = halo_send.shape[0] // 2
    total = own + 2 * halo
    bits = patches.bit_length() - 1
    chunks = [slice(i, i + chunk) for i in range(0, edges, chunk)]

    def bit_of(k):
        return lax.rem(lax.div(patch, jnp.int32(1 << k)), jnp.int32(2))

    def across(group, flips):
        there = patch
        for i, k in enumerate(group):
            if (flips >> i) & 1:
                there = there + (1 - 2 * bit_of(k)) * (1 << k)
        return there

    def part_of(group, flips):
        place = 0
        for i, k in enumerate(group):
            bit = bit_of(k)
            place = 2 * place + (1 - bit if (flips >> i) & 1 else bit)
        return place

    greet = [(patch, other), (nxt, core), (prv, core)]
    for group in make_phases(bits)[0]:
        greet += [(across(group, flips), core) for flips in range(1, 1 << len(group))]
    barrier = pltpu.get_barrier_semaphore()
    for target in greet:
        pl.semaphore_signal(barrier, inc=1, device_id=target, device_id_type=MESH)

    mine = pl.ds(pl.multiple_of(halo + core * node_rows, 16), node_rows)
    own_nodes = pl.ds(pl.multiple_of(core * node_rows, 16), node_rows)
    away_nodes = pl.ds(pl.multiple_of(other * node_rows, 16), node_rows)
    inner = slice(halo, halo + own)

    loads = {}
    for k, (name, src, dst) in enumerate(
        (
            ("node", node_hbm, ext.at[mine]),
            ("edge", edge_hbm, edge_ref),
            ("a", a_hbm, a_ref),
            ("b", b_hbm, b_ref),
            ("gn", gn_hbm, gn_ref.at[own_nodes]),
            ("na", na_hbm, na_ref),
            ("nb", nb_hbm, nb_ref),
            ("ge", ge_hbm, ge_ref),
        )
    ):
        loads[name] = pltpu.make_async_copy(src, dst, in_sem.at[k])
        loads[name].start()

    pl.semaphore_wait(barrier, len(greet))

    started = []

    def send(src, dst, target):
        k = len(started)
        copy = pltpu.make_async_remote_copy(
            src_ref=src, dst_ref=dst, send_sem=send_sem.at[k], recv_sem=recv_sem.at[k],
            device_id=target, device_id_type=MESH,
        )
        copy.start()
        started.append(copy)
        return copy

    to_core = send(node_hbm, ext.at[mine], (patch, other))
    to_core_grad = send(gn_hbm, gn_ref.at[own_nodes], (patch, other))

    state = []
    for k, phases in enumerate(make_phases(bits)):
        bufs = buffers[k * (2 + len(phases)) : (k + 1) * (2 + len(phases))]
        order = [b for group in phases for b in group]
        state.append(
            dict(phases=phases, order=order, bufs=bufs, copies=[], step=0, base=0, left=patches, out=k * half)
        )

    def gradient(k, left_t, right):
        job = state[k]
        block = job["bufs"][0]
        for side in (other, core):
            lanes = pl.ds(pl.multiple_of(side * half, LANES), half)
            value = times(left_t, right(lanes)).astype(bf16)
            for p in range(patches):
                where = sum(((p >> b) & 1) << (bits - 1 - i) for i, b in enumerate(job["order"]))
                block[side, where] = value[p * rows_out : (p + 1) * rows_out]
            if side is other:
                job["copies"] = [send(block.at[other], job["bufs"][1], (patch, other))]

    def advance(*ks):
        for k in ks:
            job = state[k]
            step, base, block, phases = job["step"], job["base"], job["bufs"][0], job["phases"]
            if step > len(phases):
                continue
            buf = job["bufs"][1 + step]
            got = [buf] if step == 0 else [buf.at[i] for i in range(buf.shape[0])]
            for copy in job["copies"]:
                copy.wait_recv()
            if step == len(phases):
                value = block[core, base].astype(f32)
                for part in got:
                    value += part[0].astype(f32)
                fin[core, :, job["out"] : job["out"] + half] = value
            else:
                group = phases[step]
                count = job["left"] >> len(group)

                def add(start):
                    where = pl.ds(base + start, count)
                    value = block[core, where].astype(f32)
                    for part in got:
                        value += part[pl.ds(start, count)].astype(f32)
                    block[core, where] = value.astype(bf16)

                job["copies"] = []
                for flips in range(1, 1 << len(group)):
                    start = part_of(group, flips) * count
                    add(start)
                    job["copies"].append(
                        send(
                            block.at[core, pl.ds(base + start, count)],
                            job["bufs"][2 + step].at[flips - 1],
                            (across(group, flips), core),
                        )
                    )
                start = part_of(group, 0) * count
                add(start)
                job["base"], job["left"] = base + start, count
            job["step"] = step + 1

    def tiles(rows, work):
        def step(i, carry):
            work(pl.ds(pl.multiple_of(i * TILE, TILE), TILE))
            return carry

        lax.fori_loop(0, rows // TILE, step, 0, unroll=4)

    hot_r[...] = lanes_hot(rcv_ref[...], own)
    loads["edge"].wait()
    loads["a"].wait()
    for rows in chunks:
        pre[rows, :] = times(edge_ref[rows, :], a_ref[:width, :])
    loads["node"].wait()
    to_core.wait_recv()
    halo_send[...] = times(lanes_hot(halo_ref[...], own), ext[inner, :]).astype(bf16)
    to_prev = send(halo_send.at[pl.ds(0, halo)], ext.at[pl.ds(halo + own, halo)], (prv, core))
    to_next = send(halo_send.at[pl.ds(halo, halo)], ext.at[pl.ds(0, halo)], (nxt, core))

    for rows in chunks:
        taken = times(hot_r[rows, :], ext[inner, :]).astype(bf16)
        pre[rows, :] += times(taken, a_ref[2 * width :, :])
    hot_s[...] = lanes_hot(snd_ref[...], total)
    loads["b"].wait()
    to_prev.wait_recv()
    to_next.wait_recv()
    for rows in chunks:
        taken = times(hot_s[rows, :], ext[...]).astype(bf16)
        pre[rows, :] += times(taken, a_ref[width : 2 * width, :])

    def activate(rows):
        value = pre[rows, :]
        act[rows, :] = (value * jax.nn.sigmoid(value)).astype(bf16)

    tiles(edges, activate)
    for rows in chunks:
        normed[rows, :] = times(act[rows, :], b_ref[...])

    def normalize(rows):
        scaled, scale = layer_norm(normed[rows, :])
        normed[rows, :] = scaled
        inv[rows, :] = scale
        updated[rows, :] = (edge_ref[rows, :].astype(f32) + scaled).astype(bf16)

    tiles(edges, normalize)
    agg_send[...] = times(rows_hot(rcv_ref[...], own), updated[...]).astype(bf16)
    to_agg = send(agg_send, agg_recv, (patch, other))

    def slope(rows):
        pre[rows, :] = swish_slope(pre[rows, :])

    tiles(edges, slope)
    for name in ("na", "nb", "gn", "ge"):
        loads[name].wait()
    to_core_grad.wait_recv()
    to_agg.wait_recv()

    node = ext[inner, :]
    aggregate = (agg_send[...].astype(f32) + agg_recv[...].astype(f32)).astype(bf16)
    agg[...] = aggregate
    n_pre[...] = times(node, na_ref[:width, :]) + times(aggregate, na_ref[width:, :])

    def node_activate(rows):
        value = n_pre[rows, :]
        sig = jax.nn.sigmoid(value)
        n_act[rows, :] = (value * sig).astype(bf16)
        n_pre[rows, :] = sig * (1.0 + value * (1.0 - sig))

    tiles(own, node_activate)
    n_out[...] = times(n_act[...], nb_ref[...])

    def node_norm(rows):
        scaled, scale = layer_norm(n_out[rows, :])
        n_dout[rows, :] = norm_backward(gn_ref[rows, :].astype(f32), scaled, scale)

    tiles(own, node_norm)
    d_pre = (times_transpose(n_dout[...], nb_ref[...]) * n_pre[...]).astype(bf16)
    n_dpre[...] = d_pre
    spread[...] = times_transpose(d_pre, na_ref[width:, :]).astype(bf16)

    n_dpre_own = n_dpre[own_nodes, :]
    n_dpre_t = n_dpre_own.T
    gradient(0, n_dpre_t, lambda lanes: ext[mine, lanes])
    gradient(1, n_dpre_t, lambda lanes: agg[own_nodes, lanes])
    gradient(2, n_dout[own_nodes, :].T, lambda lanes: n_act[own_nodes, lanes])

    for rows in chunks:
        cot[rows, :] = times(hot_r[rows, :], spread[...])

    def edge_cotangent(rows):
        cotangent = ge_ref[rows, :].astype(f32) + cot[rows, :]
        cot[rows, :] = cotangent
        dout[rows, :] = norm_backward(cotangent, normed[rows, :], inv[rows, :])

    tiles(edges, edge_cotangent)
    advance(0, 1, 2)
    gradient(3, dout[...].T, lambda lanes: act[:, lanes])
    for rows in chunks:
        dpre[rows, :] = (times_transpose(dout[rows, :], b_ref[...]) * pre[rows, :]).astype(bf16)
    dpre_t[...] = dpre[...].T
    advance(3)
    gradient(4, dpre_t[...], lambda lanes: edge_ref[:, lanes])
    from_s_t = times(dpre_t[...], hot_s[...]).astype(bf16)
    gradient(5, from_s_t, lambda lanes: ext[:, lanes])
    from_r_t = times(dpre_t[...], hot_r[...]).astype(bf16)
    gradient(6, from_r_t, lambda lanes: ext[inner, lanes])
    advance(4, 0, 1, 2)

    from_s = from_s_t.T
    from_r = from_r_t.T
    back_send[:halo, :] = times_transpose(from_s[:halo, :], a_ref[width : 2 * width, :]).astype(bf16)
    back_send[halo:, :] = times_transpose(from_s[halo + own :, :], a_ref[width : 2 * width, :]).astype(bf16)
    back_prev = send(back_send.at[pl.ds(0, halo)], back_recv.at[pl.ds(halo, halo)], (prv, core))
    back_next = send(back_send.at[pl.ds(halo, halo)], back_recv.at[pl.ds(0, halo)], (nxt, core))
    advance(5, 6)
    stores = []

    def edge_rows(k):
        rows = chunks[k]
        gedge[rows, :] = (cot[rows, :] + times_transpose(dpre[rows, :], a_ref[:width, :])).astype(bf16)
        stores.append(pltpu.make_async_copy(gedge.at[rows], gedge_hbm.at[rows], out_sem.at[k]))
        stores[-1].start()

    split = len(chunks) // 2
    for k in range(split):
        edge_rows(k)
    advance(3, 4, 0, 1, 2)
    for k in range(split, len(chunks)):
        edge_rows(k)
    own_acc[...] = times_transpose(from_s[inner, :], a_ref[width : 2 * width, :]) + times_transpose(
        from_r, a_ref[2 * width :, :]
    )
    dnode[...] = gn_ref[own_nodes, :].astype(f32) + times_transpose(n_dpre_own, na_ref[:width, :])
    advance(5, 6, 3, 4)
    back_prev.wait_recv()
    back_next.wait_recv()
    own_acc[...] += times(rows_hot(halo_ref[...], own), back_recv[...])
    own_send[...] = own_acc[away_nodes, :].astype(bf16)
    to_own = send(own_send, own_recv, (patch, other))
    advance(5, 6, 0, 1, 2, 3, 4)
    to_own.wait_recv()
    gnode_out[...] = (own_acc[own_nodes, :] + own_recv[...].astype(f32) + dnode[...]).astype(bf16)
    for _ in range(4):
        advance(0, 1, 2, 3, 4, 5, 6)

    send(fin.at[core], fin.at[core], (patch, other)).wait_recv()
    wsum_out[...] = fin[...]
    for copy in stores:
        copy.wait()
    for copy in started:
        copy.wait_send()


def finish_kernel(half, gnode_ref, gedge_ref, wsum_ref, gnode_out, gedge_out, e1, e2, n1, n2, sem):
    copies = [(gedge_ref, gedge_out), (gnode_ref, gnode_out)]
    outs = {"edge_first": e1, "edge_second": e2, "node_first": n1, "node_second": n2}
    seen = {name: 0 for name in outs}
    for k, name in enumerate(JOBS):
        for side in range(2):
            low = seen[name] + side * half
            copies.append((wsum_ref.at[side, :, k * half : (k + 1) * half], outs[name].at[:, low : low + half]))
        seen[name] += 2 * half
    copies = [pltpu.make_async_copy(src, dst, sem.at[k]) for k, (src, dst) in enumerate(copies)]
    for copy in copies:
        copy.start()
    for copy in copies:
        copy.wait()


def fused_body(
    node_latent,
    edge_latent,
    senders,
    receivers,
    halo_list,
    w_edge_first,
    w_edge_second,
    w_node_first,
    w_node_second,
    grad_node_new,
    grad_edge_new,
):
    patches = lax.axis_size("patch")
    edges, width = edge_latent.shape
    node_rows = node_latent.shape[0]
    units = w_edge_first.shape[1]
    half = width // 2
    chunk = edges // 2
    halo2 = halo_list.shape[1]
    own = 2 * node_rows
    total = own + halo2
    rows_out = units // patches
    bits = patches.bit_length() - 1
    cfg = dict(patches=patches, rows_out=rows_out, half=half, chunk=chunk)
    job_bufs = []
    copies = 9
    for phases in make_phases(bits):
        shape = (rows_out, half)
        job_bufs.append(pltpu.VMEM((2, patches) + shape, bf16))
        job_bufs.append(pltpu.VMEM((patches,) + shape, bf16))
        left = patches
        copies += 1
        for group in phases:
            left >>= len(group)
            job_bufs.append(pltpu.VMEM(((1 << len(group)) - 1, left) + shape, bf16))
            copies += (1 << len(group)) - 1
    scratch = [
        pltpu.VMEM(edge_latent.shape, bf16),
        pltpu.VMEM(w_edge_first.shape, bf16),
        pltpu.VMEM(w_edge_second.shape, bf16),
        pltpu.VMEM(w_node_first.shape, bf16),
        pltpu.VMEM(w_node_second.shape, bf16),
        pltpu.VMEM((own, width), bf16),
        pltpu.VMEM((edges, width), bf16),
        pltpu.VMEM((total, width), bf16),
        pltpu.VMEM((edges, total), bf16),
        pltpu.VMEM((edges, own), bf16),
        pltpu.VMEM((edges, units), f32),
        pltpu.VMEM((edges, units), bf16),
        pltpu.VMEM((edges, width), f32),
        pltpu.VMEM((edges, 1), f32),
        pltpu.VMEM((edges, width), f32),
        pltpu.VMEM((edges, width), bf16),
        pltpu.VMEM((edges, units), bf16),
        pltpu.VMEM((units, edges), bf16),
        pltpu.VMEM((edges, width), bf16),
        pltpu.VMEM((edges, width), bf16),
        pltpu.VMEM((halo2, width), bf16),
        pltpu.VMEM((own, width), bf16),
        pltpu.VMEM((own, width), bf16),
        pltpu.VMEM((own, width), bf16),
        pltpu.VMEM((own, units), bf16),
        pltpu.VMEM((own, width), bf16),
        pltpu.VMEM((own, units), bf16),
        pltpu.VMEM((own, units), f32),
        pltpu.VMEM((own, width), f32),
        pltpu.VMEM((own, width), bf16),
        pltpu.VMEM((node_rows, width), f32),
        pltpu.VMEM((halo2, width), bf16),
        pltpu.VMEM((halo2, width), bf16),
        pltpu.VMEM((own, width), f32),
        pltpu.VMEM((node_rows, width), bf16),
        pltpu.VMEM((node_rows, width), bf16),
        pltpu.VMEM((2, rows_out, len(JOBS) * half), f32),
        pltpu.SemaphoreType.DMA((8,)),
        pltpu.SemaphoreType.DMA((edges // chunk,)),
        pltpu.SemaphoreType.DMA((copies,)),
        pltpu.SemaphoreType.DMA((copies,)),
    ] + job_bufs
    vmem = pl.BlockSpec(memory_space=pltpu.VMEM)
    hbm = pl.BlockSpec(memory_space=pltpu.HBM)
    anywhere = pl.BlockSpec(memory_space=pl.ANY)
    gnode, gedge, wsum = pl.pallas_call(
        functools.partial(fused_kernel, cfg),
        out_shape=[
            jax.ShapeDtypeStruct((node_rows, width), bf16),
            jax.ShapeDtypeStruct((edges, width), bf16),
            jax.ShapeDtypeStruct((2, rows_out, len(JOBS) * half), f32),
        ],
        in_specs=[hbm, hbm, vmem, vmem, vmem] + [hbm] * 6,
        out_specs=[vmem, anywhere, vmem],
        scratch_shapes=scratch,
        compiler_params=pltpu.CompilerParams(
            collective_id=0, has_side_effects=True, vmem_limit_bytes=56 * 1024 * 1024
        ),
        name="layer_backward",
    )(
        node_latent,
        edge_latent,
        senders.reshape(1, edges),
        receivers.reshape(1, edges),
        halo_list,
        w_edge_first,
        w_edge_second,
        w_node_first,
        w_node_second,
        grad_node_new,
        grad_edge_new,
    )
    matrices = (w_edge_first, w_edge_second, w_node_first, w_node_second)
    gnode, gedge, *parts = pl.pallas_call(
        functools.partial(finish_kernel, half),
        out_shape=[
            jax.ShapeDtypeStruct((node_rows, width), bf16),
            jax.ShapeDtypeStruct((edges, width), bf16),
        ]
        + [jax.ShapeDtypeStruct((rows_out, m.shape[0]), f32) for m in matrices],
        in_specs=[vmem] * 3,
        out_specs=[hbm] * 6,
        scratch_shapes=[pltpu.SemaphoreType.DMA((2 + 2 * len(JOBS),))],
        name="results",
    )(gnode, gedge, wsum)
    return (gnode, gedge) + tuple(part.T for part in parts)


def solution(mesh):
    in_specs = (
        P(("patch", "shard"), None),
        P(("patch", "shard"), None),
        P(("patch", "shard")),
        P(("patch", "shard")),
        P("patch", None),
        P(),
        P(),
        P(),
        P(),
        P(("patch", "shard"), None),
        P(("patch", "shard"), None),
    )
    out_specs = (
        P(("patch", "shard"), None),
        P(("patch", "shard"), None),
        P(None, "patch"),
        P(None, "patch"),
        P(None, "patch"),
        P(None, "patch"),
    )
    patches, shards = mesh.shape["patch"], mesh.shape["shard"]
    covered = shards == 2 and patches >= 4 and patches & (patches - 1) == 0
    body = fused_body if covered else general_body
    return jax.shard_map(body, mesh=mesh, in_specs=in_specs, out_specs=out_specs, check_vma=False)
```

```python
import functools

import jax
import jax.numpy as jnp
from jax import lax
from jax.experimental import pallas as pl
from jax.experimental.pallas import tpu as pltpu
from jax.sharding import PartitionSpec as P

epsilon = 1e-05
LANES = 128
TILE = 32
bf16 = jnp.bfloat16
f32 = jnp.float32
MESH = pl.DeviceIdType.MESH


def padded(block, sides, width):
    for axis, dim in sides:
        count = lax.axis_size(axis)
        forward = [(i, i + 1) for i in range(count - 1)]
        forward.append((count - 1, 0))
        backward = [(target, source) for source, target in forward]
        low = lax.ppermute(
            lax.slice_in_dim(block, block.shape[dim] - width, None, axis=dim), axis, forward
        )
        high = lax.ppermute(lax.slice_in_dim(block, 0, width, axis=dim), axis, backward)
        block = jnp.concatenate([low, block, high], axis=dim)
    return block


def swish_slope(values):
    sig = jax.nn.sigmoid(values)
    return sig * (1.0 + values * (1.0 - sig))


def contract_rows(left, right):
    return lax.dot_general(
        left, right, (((0,), (0,)), ((), ())), preferred_element_type=jnp.float32
    )


def times_transpose(left, right):
    return lax.dot_general(
        left, right, (((1,), (1,)), ((), ())), preferred_element_type=jnp.float32
    )


def times(left, right):
    return jnp.dot(left, right, preferred_element_type=jnp.float32)


def layer_norm(output):
    center = output - jnp.mean(output, axis=-1, keepdims=True)
    inv_scale = lax.rsqrt(jnp.mean(center * center, axis=-1, keepdims=True) + epsilon)
    return center * inv_scale, inv_scale


def norm_backward(cotangent, normed, inv_scale):
    return (
        inv_scale
        * (
            cotangent
            - jnp.mean(cotangent, axis=-1, keepdims=True)
            - normed * jnp.mean(cotangent * normed, axis=-1, keepdims=True)
        )
    ).astype(bf16)


def mlp_forward(joined, w_first, w_second):
    pre_act = times(joined, w_first)
    activated = (pre_act * jax.nn.sigmoid(pre_act)).astype(jnp.bfloat16)
    normed, inv_scale = layer_norm(times(activated, w_second))
    return (pre_act, activated, normed, inv_scale)


def mlp_backward(joined, w_first, w_second, pre_act, activated, normed, inv_scale, cotangent):
    d_out = norm_backward(cotangent, normed, inv_scale)
    d_act = times_transpose(d_out, w_second)
    d_pre = (d_act * swish_slope(pre_act)).astype(jnp.bfloat16)
    grad_second = contract_rows(activated, d_out)
    grad_first = contract_rows(joined, d_pre)
    d_joined = times_transpose(d_pre, w_first)
    return (d_joined, grad_first, grad_second)


def general_body(
    node_latent,
    edge_latent,
    senders,
    receivers,
    halo_list,
    w_edge_first,
    w_edge_second,
    w_node_first,
    w_node_second,
    grad_node_new,
    grad_edge_new,
):
    shards = lax.axis_size("shard")
    node_rows = node_latent.shape[0]
    width = node_latent.shape[1]
    patch_rows = node_rows * shards
    send_lists = halo_list[0]
    halo_width = send_lists.shape[0] // 2
    gathered = lax.all_gather(node_latent, "shard", axis=0, tiled=True)
    outgoing = jnp.take(gathered, send_lists, axis=0)
    widened = padded(outgoing, (("patch", 0),), halo_width)
    from_prev = widened[:halo_width]
    from_next = widened[halo_width * 3 :]
    extended = jnp.concatenate([from_prev, gathered, from_next], axis=0)
    joined = jnp.concatenate(
        [edge_latent, jnp.take(extended, senders, axis=0), jnp.take(gathered, receivers, axis=0)],
        axis=1,
    )
    pre_act, activated, normed, inv_scale = mlp_forward(joined, w_edge_first, w_edge_second)
    edge_new = (edge_latent.astype(jnp.float32) + normed).astype(jnp.bfloat16)
    partial_value = jax.ops.segment_sum(
        edge_new.astype(jnp.float32), receivers, num_segments=patch_rows
    )
    aggregate = lax.psum_scatter(
        partial_value.astype(jnp.bfloat16), "shard", scatter_dimension=0, tiled=True
    )
    node_joined = jnp.concatenate([node_latent, aggregate], axis=1)
    n_pre, n_act, n_normed, n_inv = mlp_forward(node_joined, w_node_first, w_node_second)
    node_grad = grad_node_new.astype(jnp.float32)
    d_node, g_node_first, g_node_second = mlp_backward(
        node_joined, w_node_first, w_node_second, n_pre, n_act, n_normed, n_inv, node_grad
    )
    d_aggregate = d_node[:, width:]
    spread = lax.all_gather(d_aggregate.astype(jnp.bfloat16), "shard", axis=0, tiled=True).astype(
        d_aggregate.dtype
    )
    edge_grad = grad_edge_new.astype(jnp.float32) + jnp.take(spread, receivers, axis=0)
    d_edge, g_edge_first, g_edge_second = mlp_backward(
        joined, w_edge_first, w_edge_second, pre_act, activated, normed, inv_scale, edge_grad
    )
    grad_edge_latent = (edge_grad + d_edge[:, :width]).astype(jnp.bfloat16)
    sender_part = jax.ops.segment_sum(
        d_edge[:, width : 2 * width], senders, num_segments=patch_rows + 2 * halo_width
    )
    receiver_part = jax.ops.segment_sum(d_edge[:, 2 * width :], receivers, num_segments=patch_rows)
    back_part = jnp.concatenate(
        [sender_part[:halo_width], sender_part[halo_width + patch_rows :]], axis=0
    )
    returned = padded(back_part.astype(jnp.bfloat16), (("patch", 0),), halo_width).astype(
        back_part.dtype
    )
    own_rows = sender_part[halo_width : halo_width + patch_rows] + receiver_part
    own_rows = own_rows.at[send_lists[:halo_width]].add(returned[:halo_width])
    own_rows = own_rows.at[send_lists[halo_width:]].add(returned[halo_width * 3 :])
    node_total = lax.psum_scatter(
        own_rows.astype(jnp.bfloat16), "shard", scatter_dimension=0, tiled=True
    ).astype(jnp.float32)
    grad_node_latent = (node_total + node_grad + d_node[:, :width]).astype(jnp.bfloat16)
    summed = lax.psum(
        (g_edge_first, g_edge_second, g_node_first, g_node_second), ("patch", "shard")
    )
    patches = lax.axis_size("patch")
    patch_index = lax.axis_index("patch")
    sliced = tuple(
        (
            lax.dynamic_slice_in_dim(
                matrix, patch_index * (matrix.shape[1] // patches), matrix.shape[1] // patches, 1
            )
            for matrix in summed
        )
    )
    return (grad_node_latent, grad_edge_latent, sliced[0], sliced[1], sliced[2], sliced[3])


def rows_hot(index_row, count):
    k = index_row.shape[1]
    return (lax.broadcasted_iota(jnp.int32, (count, k), 0) == index_row).astype(f32).astype(bf16)


def lanes_hot(index_row, count):
    k = index_row.shape[1]
    column = jnp.broadcast_to(index_row, (LANES, k)).T
    lane = lax.broadcasted_iota(jnp.int32, (k, LANES), 1)
    parts = [(column == lane + base).astype(f32).astype(bf16) for base in range(0, count, LANES)]
    return jnp.concatenate(parts, axis=1)


JOBS = ("node_first", "node_first", "node_second", "edge_second", "edge_first", "edge_first", "edge_first")


def make_phases(bits):
    upper = list(range(2, bits))
    first = ([0], [1], upper)
    second = ([1], [0], upper)
    third = (upper, [0], [1])
    return (first, second, first, third, first, second, second)


def fused_kernel(cfg, *refs):
    patches, rows_out, half, chunk = cfg["patches"], cfg["rows_out"], cfg["half"], cfg["chunk"]
    (node_hbm, edge_hbm, snd_ref, rcv_ref, halo_ref, a_hbm, b_hbm, na_hbm, nb_hbm, gn_hbm, ge_hbm) = refs[:11]
    gnode_out, gedge_hbm, wsum_out = refs[11:14]
    (edge_ref, a_ref, b_ref, na_ref, nb_ref, gn_ref, ge_ref,
     ext, hot_s, hot_r, pre, act, normed, inv, cot, dout, dpre, dpre_t, updated, gedge,
     halo_send, agg_send, agg_recv, agg, n_dpre, n_dout, n_act, shares, spread, dnode,
     back_send, back_recv, own_acc, own_send, own_recv, fin,
     in_sem, out_sem, send_sem, recv_sem) = refs[14:54]
    buffers = refs[54:]

    patch = lax.axis_index("patch")
    core = lax.axis_index("shard")
    other = 1 - core
    nxt = lax.rem(patch + 1, patches)
    prv = lax.rem(patch + patches - 1, patches)
    node_rows, width = node_hbm.shape
    edges = edge_hbm.shape[0]
    own = 2 * node_rows
    halo = halo_send.shape[0] // 2
    total = own + 2 * halo
    bits = patches.bit_length() - 1
    chunks = [slice(i, i + chunk) for i in range(0, edges, chunk)]

    def bit_of(k):
        return lax.rem(lax.div(patch, jnp.int32(1 << k)), jnp.int32(2))

    def across(group, flips):
        there = patch
        for i, k in enumerate(group):
            if (flips >> i) & 1:
                there = there + (1 - 2 * bit_of(k)) * (1 << k)
        return there

    def part_of(group, flips):
        place = 0
        for i, k in enumerate(group):
            bit = bit_of(k)
            place = 2 * place + (1 - bit if (flips >> i) & 1 else bit)
        return place

    greet = [(patch, other), (nxt, core), (prv, core)]
    for group in make_phases(bits)[0]:
        greet += [(across(group, flips), core) for flips in range(1, 1 << len(group))]
    barrier = pltpu.get_barrier_semaphore()
    for target in greet:
        pl.semaphore_signal(barrier, inc=1, device_id=target, device_id_type=MESH)

    mine = pl.ds(pl.multiple_of(halo + core * node_rows, 16), node_rows)
    own_nodes = pl.ds(pl.multiple_of(core * node_rows, 16), node_rows)
    away_nodes = pl.ds(pl.multiple_of(other * node_rows, 16), node_rows)
    inner = slice(halo, halo + own)

    loads = {}
    for k, (name, src, dst) in enumerate(
        (
            ("node", node_hbm, ext.at[mine]),
            ("edge", edge_hbm, edge_ref),
            ("a", a_hbm, a_ref),
            ("b", b_hbm, b_ref),
            ("gn", gn_hbm, gn_ref.at[own_nodes]),
            ("na", na_hbm, na_ref),
            ("nb", nb_hbm, nb_ref),
            ("ge", ge_hbm, ge_ref),
        )
    ):
        loads[name] = pltpu.make_async_copy(src, dst, in_sem.at[k])
        loads[name].start()

    pl.semaphore_wait(barrier, len(greet))

    started = []

    def send(src, dst, target):
        k = len(started)
        copy = pltpu.make_async_remote_copy(
            src_ref=src, dst_ref=dst, send_sem=send_sem.at[k], recv_sem=recv_sem.at[k],
            device_id=target, device_id_type=MESH,
        )
        copy.start()
        started.append(copy)
        return copy

    to_core = send(node_hbm, ext.at[mine], (patch, other))
    to_core_grad = send(gn_hbm, gn_ref.at[own_nodes], (patch, other))

    state = []
    for k, phases in enumerate(make_phases(bits)):
        bufs = buffers[k * (2 + len(phases)) : (k + 1) * (2 + len(phases))]
        order = [b for group in phases for b in group]
        state.append(
            dict(phases=phases, order=order, bufs=bufs, copies=[], step=0, base=0, left=patches, out=k * half)
        )

    def gradient(k, left_t, right):
        job = state[k]
        block = job["bufs"][0]
        for side in (other, core):
            lanes = pl.ds(pl.multiple_of(side * half, LANES), half)
            value = times(left_t, right(lanes)).astype(bf16)
            for p in range(patches):
                where = sum(((p >> b) & 1) << (bits - 1 - i) for i, b in enumerate(job["order"]))
                block[side, where] = value[p * rows_out : (p + 1) * rows_out]
            if side is other:
                job["copies"] = [send(block.at[other], job["bufs"][1], (patch, other))]

    def advance(*ks):
        for k in ks:
            job = state[k]
            step, base, block, phases = job["step"], job["base"], job["bufs"][0], job["phases"]
            if step > len(phases):
                continue
            buf = job["bufs"][1 + step]
            got = [buf] if step == 0 else [buf.at[i] for i in range(buf.shape[0])]
            for copy in job["copies"]:
                copy.wait_recv()
            if step == len(phases):
                value = block[core, base].astype(f32)
                for part in got:
                    value += part[0].astype(f32)
                fin[core, :, job["out"] : job["out"] + half] = value
            else:
                group = phases[step]
                count = job["left"] >> len(group)

                def add(start):
                    where = pl.ds(base + start, count)
                    value = block[core, where].astype(f32)
                    for part in got:
                        value += part[pl.ds(start, count)].astype(f32)
                    block[core, where] = value.astype(bf16)

                job["copies"] = []
                for flips in range(1, 1 << len(group)):
                    start = part_of(group, flips) * count
                    add(start)
                    job["copies"].append(
                        send(
                            block.at[core, pl.ds(base + start, count)],
                            job["bufs"][2 + step].at[flips - 1],
                            (across(group, flips), core),
                        )
                    )
                start = part_of(group, 0) * count
                add(start)
                job["base"], job["left"] = base + start, count
            job["step"] = step + 1

    def tiles(rows, work):
        def step(i, carry):
            work(pl.ds(pl.multiple_of(i * TILE, TILE), TILE))
            return carry

        lax.fori_loop(0, rows // TILE, step, 0, unroll=4)

    hot_r[...] = lanes_hot(rcv_ref[...], own)
    loads["edge"].wait()
    loads["a"].wait()
    for rows in chunks:
        pre[rows, :] = times(edge_ref[rows, :], a_ref[:width, :])
    loads["node"].wait()
    to_core.wait_recv()
    halo_send[...] = times(lanes_hot(halo_ref[...], own), ext[inner, :]).astype(bf16)
    to_prev = send(halo_send.at[pl.ds(0, halo)], ext.at[pl.ds(halo + own, halo)], (prv, core))
    to_next = send(halo_send.at[pl.ds(halo, halo)], ext.at[pl.ds(0, halo)], (nxt, core))

    shares[:own, :] = times(ext[inner, :], a_ref[2 * width :, :]).astype(bf16)
    for rows in chunks:
        pre[rows, :] += times(hot_r[rows, :], shares[:own, :])
    hot_s[...] = lanes_hot(snd_ref[...], total)
    loads["b"].wait()
    to_prev.wait_recv()
    to_next.wait_recv()
    shares[...] = times(ext[...], a_ref[width : 2 * width, :]).astype(bf16)
    for rows in chunks:
        value = pre[rows, :] + times(hot_s[rows, :], shares[...])
        pre[rows, :] = value
        hidden = (value * jax.nn.sigmoid(value)).astype(bf16)
        act[rows, :] = hidden
        scaled, scale = layer_norm(times(hidden, b_ref[...]))
        normed[rows, :] = scaled
        inv[rows, :] = scale
        updated[rows, :] = (edge_ref[rows, :].astype(f32) + scaled).astype(bf16)
    agg_send[...] = times(rows_hot(rcv_ref[...], own), updated[...]).astype(bf16)
    to_agg = send(agg_send, agg_recv, (patch, other))

    def slope(rows):
        pre[rows, :] = swish_slope(pre[rows, :])

    tiles(edges, slope)
    for name in ("na", "nb", "gn", "ge"):
        loads[name].wait()
    to_core_grad.wait_recv()
    to_agg.wait_recv()

    node = ext[inner, :]
    aggregate = (agg_send[...].astype(f32) + agg_recv[...].astype(f32)).astype(bf16)
    agg[...] = aggregate
    n_pre = times(node, na_ref[:width, :]) + times(aggregate, na_ref[width:, :])
    hidden = (n_pre * jax.nn.sigmoid(n_pre)).astype(bf16)
    n_act[...] = hidden
    n_normed, n_inv = layer_norm(times(hidden, nb_ref[...]))
    d_out = norm_backward(gn_ref[...].astype(f32), n_normed, n_inv)
    n_dout[...] = d_out
    d_pre = (times_transpose(d_out, nb_ref[...]) * swish_slope(n_pre)).astype(bf16)
    n_dpre[...] = d_pre
    spread[...] = times_transpose(d_pre, na_ref[width:, :]).astype(bf16)

    n_dpre_own = n_dpre[own_nodes, :]
    n_dpre_t = n_dpre_own.T
    gradient(0, n_dpre_t, lambda lanes: ext[mine, lanes])
    gradient(1, n_dpre_t, lambda lanes: agg[own_nodes, lanes])
    gradient(2, n_dout[own_nodes, :].T, lambda lanes: n_act[own_nodes, lanes])

    for rows in chunks:
        cotangent = ge_ref[rows, :].astype(f32) + times(hot_r[rows, :], spread[...])
        cot[rows, :] = cotangent
        dout[rows, :] = norm_backward(cotangent, normed[rows, :], inv[rows, :])
    advance(0, 1, 2)
    gradient(3, dout[...].T, lambda lanes: act[:, lanes])
    for rows in chunks:
        dpre[rows, :] = (times_transpose(dout[rows, :], b_ref[...]) * pre[rows, :]).astype(bf16)
    dpre_t[...] = dpre[...].T
    advance(3)
    gradient(4, dpre_t[...], lambda lanes: edge_ref[:, lanes])
    from_s_t = times(dpre_t[...], hot_s[...]).astype(bf16)
    gradient(5, from_s_t, lambda lanes: ext[:, lanes])
    from_r_t = times(dpre_t[...], hot_r[...]).astype(bf16)
    gradient(6, from_r_t, lambda lanes: ext[inner, lanes])
    advance(4, 0, 1, 2)

    from_s = from_s_t.T
    from_r = from_r_t.T
    back_send[:halo, :] = times_transpose(from_s[:halo, :], a_ref[width : 2 * width, :]).astype(bf16)
    back_send[halo:, :] = times_transpose(from_s[halo + own :, :], a_ref[width : 2 * width, :]).astype(bf16)
    back_prev = send(back_send.at[pl.ds(0, halo)], back_recv.at[pl.ds(halo, halo)], (prv, core))
    back_next = send(back_send.at[pl.ds(halo, halo)], back_recv.at[pl.ds(0, halo)], (nxt, core))
    advance(5, 6)
    stores = []

    def edge_rows(k):
        rows = chunks[k]
        gedge[rows, :] = (cot[rows, :] + times_transpose(dpre[rows, :], a_ref[:width, :])).astype(bf16)
        stores.append(pltpu.make_async_copy(gedge.at[rows], gedge_hbm.at[rows], out_sem.at[k]))
        stores[-1].start()

    split = len(chunks) // 2
    for k in range(split):
        edge_rows(k)
    advance(3, 4, 0, 1, 2)
    for k in range(split, len(chunks)):
        edge_rows(k)
    own_acc[...] = times_transpose(from_s[inner, :], a_ref[width : 2 * width, :]) + times_transpose(
        from_r, a_ref[2 * width :, :]
    )
    dnode[...] = gn_ref[own_nodes, :].astype(f32) + times_transpose(n_dpre_own, na_ref[:width, :])
    advance(5, 6, 3, 4)
    back_prev.wait_recv()
    back_next.wait_recv()
    own_acc[...] += times(rows_hot(halo_ref[...], own), back_recv[...])
    own_send[...] = own_acc[away_nodes, :].astype(bf16)
    to_own = send(own_send, own_recv, (patch, other))
    advance(5, 6, 0, 1, 2, 3, 4)
    to_own.wait_recv()
    gnode_out[...] = (own_acc[own_nodes, :] + own_recv[...].astype(f32) + dnode[...]).astype(bf16)
    for _ in range(4):
        advance(0, 1, 2, 3, 4, 5, 6)

    send(fin.at[core], fin.at[core], (patch, other)).wait_recv()
    wsum_out[...] = fin[...]
    for copy in stores:
        copy.wait()
    for copy in started:
        copy.wait_send()


def finish_kernel(half, gnode_ref, gedge_ref, wsum_ref, gnode_out, gedge_out, e1, e2, n1, n2, sem):
    copies = [(gedge_ref, gedge_out), (gnode_ref, gnode_out)]
    outs = {"edge_first": e1, "edge_second": e2, "node_first": n1, "node_second": n2}
    seen = {name: 0 for name in outs}
    for k, name in enumerate(JOBS):
        for side in range(2):
            low = seen[name] + side * half
            copies.append((wsum_ref.at[side, :, k * half : (k + 1) * half], outs[name].at[:, low : low + half]))
        seen[name] += 2 * half
    copies = [pltpu.make_async_copy(src, dst, sem.at[k]) for k, (src, dst) in enumerate(copies)]
    for copy in copies:
        copy.start()
    for copy in copies:
        copy.wait()


def fused_body(
    node_latent,
    edge_latent,
    senders,
    receivers,
    halo_list,
    w_edge_first,
    w_edge_second,
    w_node_first,
    w_node_second,
    grad_node_new,
    grad_edge_new,
):
    patches = lax.axis_size("patch")
    edges, width = edge_latent.shape
    node_rows = node_latent.shape[0]
    units = w_edge_first.shape[1]
    half = width // 2
    chunk = edges // 2
    halo2 = halo_list.shape[1]
    own = 2 * node_rows
    total = own + halo2
    rows_out = units // patches
    bits = patches.bit_length() - 1
    cfg = dict(patches=patches, rows_out=rows_out, half=half, chunk=chunk)
    job_bufs = []
    copies = 9
    for phases in make_phases(bits):
        shape = (rows_out, half)
        job_bufs.append(pltpu.VMEM((2, patches) + shape, bf16))
        job_bufs.append(pltpu.VMEM((patches,) + shape, bf16))
        left = patches
        copies += 1
        for group in phases:
            left >>= len(group)
            job_bufs.append(pltpu.VMEM(((1 << len(group)) - 1, left) + shape, bf16))
            copies += (1 << len(group)) - 1
    scratch = [
        pltpu.VMEM(edge_latent.shape, bf16),
        pltpu.VMEM(w_edge_first.shape, bf16),
        pltpu.VMEM(w_edge_second.shape, bf16),
        pltpu.VMEM(w_node_first.shape, bf16),
        pltpu.VMEM(w_node_second.shape, bf16),
        pltpu.VMEM((own, width), bf16),
        pltpu.VMEM((edges, width), bf16),
        pltpu.VMEM((total, width), bf16),
        pltpu.VMEM((edges, total), bf16),
        pltpu.VMEM((edges, own), bf16),
        pltpu.VMEM((edges, units), f32),
        pltpu.VMEM((edges, units), bf16),
        pltpu.VMEM((edges, width), f32),
        pltpu.VMEM((edges, 1), f32),
        pltpu.VMEM((edges, width), f32),
        pltpu.VMEM((edges, width), bf16),
        pltpu.VMEM((edges, units), bf16),
        pltpu.VMEM((units, edges), bf16),
        pltpu.VMEM((edges, width), bf16),
        pltpu.VMEM((edges, width), bf16),
        pltpu.VMEM((halo2, width), bf16),
        pltpu.VMEM((own, width), bf16),
        pltpu.VMEM((own, width), bf16),
        pltpu.VMEM((own, width), bf16),
        pltpu.VMEM((own, units), bf16),
        pltpu.VMEM((own, width), bf16),
        pltpu.VMEM((own, units), bf16),
        pltpu.VMEM((total, units), bf16),
        pltpu.VMEM((own, width), bf16),
        pltpu.VMEM((node_rows, width), f32),
        pltpu.VMEM((halo2, width), bf16),
        pltpu.VMEM((halo2, width), bf16),
        pltpu.VMEM((own, width), f32),
        pltpu.VMEM((node_rows, width), bf16),
        pltpu.VMEM((node_rows, width), bf16),
        pltpu.VMEM((2, rows_out, len(JOBS) * half), f32),
        pltpu.SemaphoreType.DMA((8,)),
        pltpu.SemaphoreType.DMA((edges // chunk,)),
        pltpu.SemaphoreType.DMA((copies,)),
        pltpu.SemaphoreType.DMA((copies,)),
    ] + job_bufs
    vmem = pl.BlockSpec(memory_space=pltpu.VMEM)
    hbm = pl.BlockSpec(memory_space=pltpu.HBM)
    anywhere = pl.BlockSpec(memory_space=pl.ANY)
    gnode, gedge, wsum = pl.pallas_call(
        functools.partial(fused_kernel, cfg),
        out_shape=[
            jax.ShapeDtypeStruct((node_rows, width), bf16),
            jax.ShapeDtypeStruct((edges, width), bf16),
            jax.ShapeDtypeStruct((2, rows_out, len(JOBS) * half), f32),
        ],
        in_specs=[hbm, hbm, vmem, vmem, vmem] + [hbm] * 6,
        out_specs=[vmem, anywhere, vmem],
        scratch_shapes=scratch,
        compiler_params=pltpu.CompilerParams(
            collective_id=0, has_side_effects=True, vmem_limit_bytes=56 * 1024 * 1024
        ),
        name="layer_backward",
    )(
        node_latent,
        edge_latent,
        senders.reshape(1, edges),
        receivers.reshape(1, edges),
        halo_list,
        w_edge_first,
        w_edge_second,
        w_node_first,
        w_node_second,
        grad_node_new,
        grad_edge_new,
    )
    matrices = (w_edge_first, w_edge_second, w_node_first, w_node_second)
    gnode, gedge, *parts = pl.pallas_call(
        functools.partial(finish_kernel, half),
        out_shape=[
            jax.ShapeDtypeStruct((node_rows, width), bf16),
            jax.ShapeDtypeStruct((edges, width), bf16),
        ]
        + [jax.ShapeDtypeStruct((rows_out, m.shape[0]), f32) for m in matrices],
        in_specs=[vmem] * 3,
        out_specs=[hbm] * 6,
        scratch_shapes=[pltpu.SemaphoreType.DMA((2 + 2 * len(JOBS),))],
        name="results",
    )(gnode, gedge, wsum)
    return (gnode, gedge) + tuple(part.T for part in parts)


def solution(mesh):
    in_specs = (
        P(("patch", "shard"), None),
        P(("patch", "shard"), None),
        P(("patch", "shard")),
        P(("patch", "shard")),
        P("patch", None),
        P(),
        P(),
        P(),
        P(),
        P(("patch", "shard"), None),
        P(("patch", "shard"), None),
    )
    out_specs = (
        P(("patch", "shard"), None),
        P(("patch", "shard"), None),
        P(None, "patch"),
        P(None, "patch"),
        P(None, "patch"),
        P(None, "patch"),
    )
    patches, shards = mesh.shape["patch"], mesh.shape["shard"]
    covered = shards == 2 and patches >= 4 and patches & (patches - 1) == 0
    body = fused_body if covered else general_body
    return jax.shard_map(body, mesh=mesh, in_specs=in_specs, out_specs=out_specs, check_vma=False)
```
